128 devices in a mesh: prompt: 8 (over x, z_hi), sample: 16 (over y, z_lo, core).
Axes of the slice: x: 4, y: 4, z: 4 (z_hi: 2, z_lo: 2; z = z_hi * 2 + z_lo), core: 2. Of those that a mesh axis runs over, the one named last changes fastest.
Arguments:
- queries: bfloat16 [256, 32, 576], P(('prompt', 'sample')), may hold values from -60 to 60
- new_keys: bfloat16 [256, 576], P(('prompt', 'sample')), may hold values from -60 to 60
- cache: bfloat16 [8, 32768, 576], P('prompt', 'sample'), may hold values from -6 to 6
- residual: bfloat16 [256, 7168], P(('prompt', 'sample')), may hold values from -1.5 to 1.5
- w_uv: bfloat16 [32, 512, 128], replicated, may hold values from -0.25 to 0.25
- w_out: bfloat16 [4096, 7168], P('sample'), may hold values from -0.09375 to 0.09375
- norm_gain: bfloat16 [7168], replicated, may hold values from 0.25 to 1.75
- router: bfloat16 [7168, 16], replicated, may hold values from -0.0625 to 0.0625
- expert_ids: int32 [256, 8], P(('prompt', 'sample')), may hold values from 0 to 15, all different within a row; in each aligned block of 2 rows (0 to 1, 2 to 3, ...) at most 2 rows name the same one
- w_gate: bfloat16 [128, 7168, 256], P(('prompt', 'sample')), may hold values from -0.0625 to 0.0625
- w_up: bfloat16 [128, 7168, 256], P(('prompt', 'sample')), may hold values from -0.0625 to 0.0625
- w_down: bfloat16 [128, 256, 7168], P(('prompt', 'sample')), may hold values from -0.125 to 0.125
- accept: int32 [8, 16], P('prompt', 'sample'), may hold values 0 or 1
- assign: int32 [8, 32], P('prompt'), may hold values from 0 to 31, each once within a row
Outputs:
- trainer_rows: bfloat16 [256, 7168], P(('prompt', 'sample'))
The draws below stay inside these ranges and needn't reach their ends.
Inputs may be any that keep to these rules, and one draw needn't show every extreme that they name: `expert_ids`: in each device's 2 rows no expert is named more than 2 times, a bound that some block reaches. `assign`: each row is a permutation of 0 to 31.
All inputs are finite; a program needn't handle non-finite values. No bound on the sum of `accept` on one device may be relied on, other than what follows from the above.
Results may differ from the reference program's by a relative error of at most 0.02.
Values may be sent and summed in bfloat16 or wider, within the bound.
A program may use at most 128 MiB of HBM per device.

```python
import math
import jax
import jax.numpy as jnp
import numpy as np
from jax import lax

D = 7168
HEADS = 32
LAT = 512
ROPE = 64
VDIM = 128
FFE = 2048
EXP_SPLIT = 8
KD = 576
UNITS = 256
TOK_DEV = 2
SAMPLES = 16
GROUP_TOK = 32
PROMPTS = 8
TOKENS = 256
PROMPT_LEN = 32768
EXPERTS = 16
TOP = 8
CAP = 2


def draw_queries(key, part):
    key = jax.random.fold_in(key, 11)
    base = jax.random.normal(key, (TOKENS, HEADS, LAT + ROPE), jnp.float32) * 3.0
    return jnp.clip(base, -60.0, 60.0).astype(jnp.bfloat16)


def draw_new_keys(key, part):
    key = jax.random.fold_in(key, 23)
    column = lax_iota_columns(LAT + ROPE)
    spread = jnp.where(column < LAT, 1.0, 12.0)
    base = jax.random.normal(key, (TOKENS, LAT + ROPE), jnp.float32)
    return jnp.clip(base * spread[None, :], -60.0, 60.0).astype(jnp.bfloat16)


def lax_iota_columns(width):
    return jnp.arange(width, dtype=jnp.int32)


def place_ends(entries, own_key, smallest, top_value):
    index_at = [jax.random.randint(jax.random.fold_in(own_key, axis), (), 0, length) for axis, length in enumerate(entries.shape)]
    longest = entries.shape.index(max(entries.shape))
    beside = index_at[:longest] + [(index_at[longest] + 1) % entries.shape[longest]] + index_at[longest + 1:]
    return entries.at[tuple(index_at)].set(smallest).at[tuple(beside)].set(top_value)


def level_of(own_key, extent, pieces, smallest, high):
    def one(dim, blocks):
        steps = jax.random.uniform(jax.random.fold_in(jax.random.fold_in(own_key, 6), dim), (blocks,), jnp.float32, smallest / len(pieces), high / len(pieces))
        return jnp.repeat(jnp.exp(steps), extent[dim] // blocks).reshape((-1,) + (1,) * (len(extent) - dim - 1))

    level = one(*pieces[0])
    for cut in pieces[1:]:
        level = level * one(*cut)
    return level


def shared_out(key, own, number, rows, amount, top, bound, slope):
    order = jax.random.permutation(key, amount)
    heavy_load, ordinary = portions_of(amount, rows * top, bound, slope, True), portions_of(amount, rows * top, bound, slope, False)
    places = jnp.arange(amount)

    def named(lengths, rotation):
        used = int((lengths > 0).sum())
        fixed = max(1, used // 4)
        passed = fixed + (places - fixed + rotation * (used - fixed)) % max(1, amount - fixed)
        return jnp.zeros((amount,), jnp.int32).at[order[jnp.where(places < fixed, places, passed)]].set(jnp.asarray(lengths, jnp.int32))

    lengths = jnp.where(number % 4 == 0, named(heavy_load, number // 4), named(ordinary, number - number // 4 - 1))
    mixed = jax.random.permutation(jax.random.fold_in(own, 3), amount)
    source_of, taker = mixed[0:amount // 2 * 2:2], mixed[1:amount // 2 * 2:2]
    room = jnp.minimum(lengths[source_of] - 1, bound - lengths[taker]) // 2
    room = jnp.where((source_of == order[0]) | (taker == order[0]) | (lengths[taker] == 0), 0, jnp.maximum(room, 0))
    passed = jax.random.randint(jax.random.fold_in(own, 4), (amount // 2,), 0, 1 << 20) % (room + 1)
    lengths = lengths.at[source_of].add(-passed).at[taker].add(passed)
    members = jnp.searchsorted(jnp.cumsum(lengths), jnp.arange(rows * top), side="right").astype(jnp.int32)
    table = members.reshape(top, rows).T
    table = table[jax.random.permutation(jax.random.fold_in(own, 1), rows)]
    rotation = jax.random.randint(jax.random.fold_in(own, 2), (rows, 1), 0, top)
    return jnp.take_along_axis(table, (jnp.arange(top)[None, :] + rotation) % top, axis=1)


def portions_of(amount, total, most, slope, full):
    portions = [(1 << 20) // math.isqrt(grade ** slope) + 1 for grade in range(1, amount + 1)]
    largest = most if full else min(most, max(-(-total // amount), total * portions[0] // sum(portions)))
    least = 1 if total - largest >= amount - 1 else 0
    holding, spare = [largest] + [least] * (amount - 1), total - largest - least * (amount - 1)
    while spare > 0:
        movable = [i for i in range(1, amount) if holding[i] < largest] or [i for i in range(1, amount) if holding[i] < most]
        mass, left = sum([portions[i] for i in movable]), spare
        for i in movable:
            addition = min(most - holding[i], max(1, left * portions[i] // mass), spare)
            holding[i] = holding[i] + addition
            spare = spare - addition
    return np.array(holding)


def centred(key, extent, scale, reach, shards=(), kind=jnp.bfloat16):
    result = jax.random.normal(key, extent, jnp.float32) * scale
    if len(shards) > 0:
        result = level_of(key, extent, shards, -0.22, 0.18) * result
    return jnp.clip(result, min=-reach, max=reach).astype(kind)


def setup_inputs(seed: int = 0) -> dict:
    keys = jax.random.split(jax.random.key(seed), 15)
    queries = draw_queries(jax.random.fold_in(keys[14], 71), 0)
    new_keys = draw_new_keys(jax.random.fold_in(keys[14], 71), 0)
    cache = centred(keys[2], (PROMPTS, PROMPT_LEN, KD), 1.0, 6.0, ((0, 8), (1, 16)))
    residual = centred(keys[3], (TOKENS, D), 0.25, 1.5, ((0, 128),))
    w_uv = centred(keys[4], (HEADS, LAT, VDIM), LAT ** -0.5, 0.25)
    w_out = centred(keys[5], (HEADS * VDIM, D), (HEADS * VDIM) ** -0.5, 0.09375, ((0, 16),))
    norm_gain = jnp.clip(1.0 + 0.15 * jax.random.normal(keys[6], (D,), jnp.float32), 0.25, 1.75).astype(jnp.bfloat16)
    router = centred(keys[7], (D, EXPERTS), D ** -0.5, 0.0625)
    expert_ids_keys = jax.random.split(jax.random.fold_in(keys[8], 1), TOKENS // TOK_DEV)
    expert_ids_turns = jax.random.permutation(jax.random.fold_in(keys[8], 3), TOKENS // TOK_DEV)
    expert_ids = jax.vmap(lambda own, number: shared_out(jax.random.fold_in(keys[8], 2), own, number, TOK_DEV, EXPERTS, TOP, CAP, 2))(expert_ids_keys, expert_ids_turns).reshape((TOKENS, TOP))
    w_gate = centred(keys[9], (EXPERTS * EXP_SPLIT, D, UNITS), D ** -0.5, 0.0625, ((0, 128),))
    w_up = centred(keys[10], (EXPERTS * EXP_SPLIT, D, UNITS), D ** -0.5, 0.0625, ((0, 128),))
    w_down = centred(keys[11], (EXPERTS * EXP_SPLIT, UNITS, D), FFE ** -0.5, 0.125, ((0, 128),))
    accept = place_ends((jax.random.randint(keys[12], (PROMPTS, SAMPLES), 0, 4) < 3).astype(jnp.int32), jax.random.fold_in(keys[12], 1), 0, 1)
    assign = jax.vmap(lambda own: jax.random.permutation(own, GROUP_TOK))(jax.random.split(keys[13], PROMPTS)).reshape((PROMPTS, GROUP_TOK)).astype(jnp.int32)
    return {"queries": queries, "new_keys": new_keys, "cache": cache, "residual": residual, "w_uv": w_uv, "w_out": w_out, "norm_gain": norm_gain, "router": router, "expert_ids": expert_ids, "w_gate": w_gate, "w_up": w_up, "w_down": w_down, "accept": accept, "assign": assign}


score_scale = 192.0 ** (-0.5)
route_scale = 2.827
norm_eps = 1e-06

def attend_group(query_group, key_group, cache_group, w_uv):
    qf = query_group.astype(jnp.float32)
    cf = cache_group.astype(jnp.float32)
    scores = jnp.einsum('ghk,lk->ghl', qf, cf) * score_scale
    own = key_group.astype(jnp.float32).reshape(SAMPLES, 2, KD)
    q_own = qf.reshape(SAMPLES, 2, HEADS, KD)
    own_scores = jnp.einsum('sthk,suk->sthu', q_own, own) * score_scale
    causal = lax.iota(jnp.int32, 2)[:, None] >= lax.iota(jnp.int32, 2)[None, :]
    causal = causal[None, :, None, :]
    own_peak = lax.optimization_barrier(jnp.max(jnp.where(causal, own_scores, -jnp.inf), axis=-1)).reshape(GROUP_TOK, HEADS)
    peak = jnp.maximum(lax.optimization_barrier(jnp.max(scores, axis=-1)), own_peak)
    weights = jnp.exp(scores - peak[..., None])
    own_weights = jnp.where(causal, jnp.exp(own_scores - peak.reshape(SAMPLES, 2, HEADS)[..., None]), 0.0)
    denom = lax.optimization_barrier(jnp.sum(weights, axis=-1)) + lax.optimization_barrier(jnp.sum(own_weights, axis=-1)).reshape(GROUP_TOK, HEADS)
    probs = weights.astype(jnp.bfloat16).astype(jnp.float32)
    own_probs = own_weights.astype(jnp.bfloat16).astype(jnp.float32)
    latent_sum = jnp.einsum('ghl,lc->ghc', probs, cf[:, :LAT])
    latent_sum = latent_sum + jnp.einsum('sthu,suc->sthc', own_probs, own[..., :LAT]).reshape(GROUP_TOK, HEADS, LAT)
    mapped = jnp.einsum('ghc,hcv->ghv', latent_sum, w_uv.astype(jnp.float32), precision=lax.Precision.HIGHEST)
    values = mapped / denom[..., None]
    return values.reshape(GROUP_TOK, HEADS * VDIM).astype(jnp.bfloat16)

def reference(queries, new_keys, cache, residual, w_uv, w_out, norm_gain, router, expert_ids, w_gate, w_up, w_down, accept, assign):

    def one_prompt(items):
        return attend_group(items[0], items[1], items[2], w_uv)
    values = lax.map(one_prompt, (queries.reshape(PROMPTS, GROUP_TOK, HEADS, KD), new_keys.reshape(PROMPTS, GROUP_TOK, KD), cache))
    values = values.reshape(TOKENS, HEADS * VDIM)
    attn = jnp.dot(values, w_out, preferred_element_type=jnp.float32)
    hidden = (residual.astype(jnp.float32) + attn).astype(jnp.bfloat16)
    hf = hidden.astype(jnp.float32)
    normed = (hf * lax.rsqrt(lax.optimization_barrier(jnp.mean(hf * hf, axis=-1, keepdims=True)) + norm_eps) * norm_gain.astype(jnp.float32)).astype(jnp.bfloat16)
    logits = jnp.dot(normed, router, preferred_element_type=jnp.float32)
    chosen_mask = jnp.any(expert_ids[:, :, None] == lax.iota(jnp.int32, EXPERTS)[None, None, :], axis=1).astype(jnp.float32)
    chosen = jax.nn.sigmoid(logits) * chosen_mask
    gate = chosen / lax.optimization_barrier(jnp.sum(chosen, axis=-1, keepdims=True)) * route_scale
    nf = normed.astype(jnp.float32)
    gate_w = w_gate.reshape(EXPERTS, EXP_SPLIT, D, UNITS)
    up_w = w_up.reshape(EXPERTS, EXP_SPLIT, D, UNITS)
    down_w = w_down.reshape(EXPERTS, EXP_SPLIT, UNITS, D)

    def one_expert(total, items):
        wg, wu, wd, column = items
        gate_part = jnp.einsum('td,jdu->jtu', nf, wg.astype(jnp.float32))
        up_part = jnp.einsum('td,jdu->jtu', nf, wu.astype(jnp.float32))
        act = (jax.nn.silu(gate_part) * up_part).astype(jnp.bfloat16).astype(jnp.float32)
        part = jnp.einsum('jtu,jud->jtd', act, wd.astype(jnp.float32)).astype(jnp.bfloat16)
        expert_out = lax.optimization_barrier(jnp.sum(part.astype(jnp.float32), axis=0))
        return (total + expert_out * column[:, None], None)
    moe, unused = lax.scan(one_expert, jnp.zeros((TOKENS, D), jnp.float32), (gate_w, up_w, down_w, gate.T))
    final = (hf + moe).astype(jnp.bfloat16)
    step_id = lax.iota(jnp.int32, TOKENS) % 2
    keep = jnp.where(step_id == 0, 1, jnp.repeat(accept.reshape(-1), 2)).astype(jnp.bfloat16)
    rows = (final * keep[:, None]).reshape(PROMPTS, GROUP_TOK, D)

    def place(rows_group, target):
        return jnp.zeros((GROUP_TOK, D), jnp.bfloat16).at[target].set(rows_group)
    return jax.vmap(place)(rows, assign).reshape(TOKENS, D)
```

```python
import functools
import jax
import jax.numpy as jnp
from jax import lax
from jax.experimental import pallas as pl
from jax.experimental.pallas import tpu as pltpu
from jax.sharding import PartitionSpec as P

MESH = pl.DeviceIdType.MESH
F32 = jnp.float32
BF16 = jnp.bfloat16
score_scale = 192.0 ** (-0.5)
log2e = 1.4426950408889634
route_scale = 2.827
norm_eps = 1e-06

COLS = 896
PIECES = ((384, 384, "xzy"), (384, 256, "yxz"), (256, 256, "zyx"))


def nt(a, b):
    return lax.dot_general(a, b, (((1,), (1,)), ((), ())), preferred_element_type=F32)


def mm(a, b):
    return jnp.dot(a, b, preferred_element_type=F32)


class Links:
    def __init__(self, send_sem, recv_sem, anyone):
        self.send_sem, self.recv_sem, self.anyone = send_sem, recv_sem, anyone
        self.sent, self.taken = [], 0

    def slots(self, n=1):
        self.taken += n
        return self.taken - n

    def send(self, src, dst, slot, device):
        copy = pltpu.make_async_remote_copy(
            src_ref=src,
            dst_ref=dst,
            send_sem=self.send_sem.at[len(self.sent)],
            recv_sem=self.recv_sem.at[slot],
            device_id=device,
            device_id_type=MESH,
        )
        copy.start()
        self.sent.append(copy)

    def arrived(self, dst, slot):
        pltpu.make_async_remote_copy(
            src_ref=dst,
            dst_ref=dst,
            send_sem=self.send_sem.at[0],
            recv_sem=self.recv_sem.at[slot],
            device_id=self.anyone,
            device_id_type=MESH,
        ).wait_recv()

    def finish(self):
        for copy in self.sent:
            copy.wait_send()


def kernel(
    q_in,
    cache_in,
    uv_in,
    out_in,
    router_in,
    gate_in,
    up_in,
    down_in,
    new_keys,
    residual,
    gain,
    ids,
    accept,
    assign,
    result,
    kc,
    wuv,
    wout,
    wgate,
    wup,
    wdown,
    rpad,
    qbuf,
    kn,
    obuf,
    vsend,
    vrecv,
    asend,
    arecv,
    hbuf,
    xa,
    xb,
    xc,
    pa,
    pb,
    pc,
    r0a,
    r0b,
    r0c,
    r1a,
    r1b,
    r1c,
    r2a,
    r2b,
    r2c,
    r3a,
    r3b,
    r3c,
    f1,
    f2,
    fsend,
    frecv,
    load_sem,
    send_sem,
    recv_sem,
):
    p = lax.axis_index("prompt")
    s = lax.axis_index("sample")
    x, zh = p // 2, p % 2
    y, zl, k = s // 4, (s // 2) % 2, s % 2
    z = zh * 2 + zl
    chip = y * 2 + zl
    at = {"x": x, "y": y, "z": z}

    def device(x, y, z, k):
        return (x * 2 + z // 2, y * 4 + (z % 2) * 2 + k)

    def peer(axis, step):
        there = dict(at)
        there[axis] = (at[axis] + step) % 4
        return device(there["x"], there["y"], there["z"], k)

    def member(t):
        return (p, t)

    other = (p, y * 4 + zl * 2 + (1 - k))
    across = (p, y * 4 + (1 - zl) * 2 + k)

    loads = []
    first_column = pl.multiple_of(chip * COLS, 128)
    for n, (src, dst) in enumerate(
        (
            (q_in, qbuf.at[s]),
            (cache_in, kc),
            (uv_in, wuv),
            (out_in, wout),
            (router_in.at[:, pl.ds(first_column, COLS)], rpad.at[pl.ds(0, 16)]),
            (gate_in, wgate),
            (up_in, wup),
            (down_in, wdown),
        )
    ):
        loads.append(pltpu.make_async_copy(src, dst, load_sem.at[n]))
        loads[-1].start()

    barrier = pltpu.get_barrier_semaphore()
    partners = [member((s + r) % 16) for r in range(1, 16)]
    partners += [peer("x", r) for r in (1, 2, 3)]
    partners += [device(x, y, (1 - zh) * 2 + r, k) for r in (0, 1)]
    for there in partners:
        pl.semaphore_signal(barrier, inc=1, device_id=there, device_id_type=MESH)
    pl.semaphore_wait(barrier, len(partners))

    links = Links(send_sem, recv_sem, other)
    send, arrived, slots = links.send, links.arrived, links.slots

    q_slot = slots(16)
    y_left, y_right, y_far = (y + 3) % 4, (y + 1) % 4, (y + 2) % 4

    def q_send(t, there):
        send(qbuf.at[t], qbuf.at[t], q_slot + t, there)

    def q_arrived(t):
        arrived(qbuf.at[t], q_slot + t)

    def q_at(yy, zz, kk):
        return yy * 4 + zz * 2 + kk

    here, beside = q_at(y, zl, k), q_at(y, 1 - zl, k)
    loads[0].wait()
    q_send(here, across)
    q_send(here, peer("y", 1))
    q_send(here, peer("y", 3))
    q_send(here, other)

    rows16 = lax.broadcasted_iota(jnp.int32, (128, 576), 0)
    fresh = new_keys[...].astype(F32)
    kn[...] = jnp.where(
        rows16 == 0, fresh[0:1, :], jnp.where(rows16 == 1, fresh[1:2, :], 0.0)
    ).astype(BF16)
    rpad[pl.ds(16, 112)] = jnp.zeros((112, COLS), BF16)

    q_arrived(beside)
    q_send(beside, peer("y", 1))
    q_send(beside, peer("y", 3))
    q_send(beside, other)
    left_own, left_beside = q_at(y_left, zl, k), q_at(y_left, 1 - zl, k)
    right_own, right_beside = q_at(y_right, zl, k), q_at(y_right, 1 - zl, k)
    far_own, far_beside = q_at(y_far, zl, k), q_at(y_far, 1 - zl, k)
    q_arrived(left_own)
    q_send(left_own, peer("y", 1))
    q_send(left_own, other)
    q_arrived(right_own)
    q_send(right_own, other)
    q_arrived(q_at(y, zl, 1 - k))
    q_arrived(q_at(y, 1 - zl, 1 - k))

    to_log2 = score_scale * log2e

    def attend(yy, own):
        q = qbuf[pl.ds(yy * 4, 4)].reshape(256, 576)
        scores = mm(q, kc[...]) * to_log2
        peak = jnp.max(scores, axis=1, keepdims=True)
        if own:
            row = lax.broadcasted_iota(jnp.int32, (256, 128), 0) - (zl * 2 + k) * 64
            column = lax.broadcasted_iota(jnp.int32, (256, 128), 1)
            seen = ((row >= 0) & (row < 64) & (column == 0)) | (
                (row >= 32) & (row < 64) & (column == 1)
            )
            own_scores = jnp.where(seen, nt(q, kn[...]) * to_log2, -jnp.inf)
            peak = jnp.maximum(peak, jnp.max(own_scores, axis=1, keepdims=True))
        weights = jnp.exp2(scores - peak)
        denom = jnp.sum(weights, axis=1, keepdims=True)
        latent = nt(weights.astype(BF16), kc[pl.ds(0, 512), :])
        if own:
            own_weights = jnp.exp2(own_scores - peak)
            denom = denom + jnp.sum(own_weights, axis=1, keepdims=True)
            latent = latent + mm(own_weights.astype(BF16), kn[:, pl.ds(0, 512)])
        at_rows = pl.ds(pl.multiple_of(yy * 256, 256), 256)
        latent = latent / denom
        for n in range(4):
            obuf[n, at_rows, :] = latent[:, n * 128 : (n + 1) * 128]
        obuf[4, at_rows, :] = jnp.broadcast_to(peak + jnp.log2(denom), (256, 128))

    loads[1].wait()
    attend(y, True)
    q_arrived(left_beside)
    q_send(left_beside, other)
    q_arrived(right_beside)
    q_send(right_beside, peer("y", 3))
    q_send(right_beside, other)
    q_arrived(q_at(y_left, zl, 1 - k))
    q_arrived(q_at(y_left, 1 - zl, 1 - k))
    attend(y_left, False)
    q_arrived(far_own)
    q_send(far_own, other)
    q_arrived(far_beside)
    q_send(far_beside, other)
    q_arrived(q_at(y_right, zl, 1 - k))
    q_arrived(q_at(y_right, 1 - zl, 1 - k))
    attend(y_right, False)
    q_arrived(q_at(y_far, zl, 1 - k))
    q_arrived(q_at(y_far, 1 - zl, 1 - k))
    attend(y_far, False)

    lane32 = lax.broadcasted_iota(jnp.int32, (32, 128), 1)
    row32 = lax.broadcasted_iota(jnp.int32, (32, 128), 0)
    facts = jnp.zeros((32, 128), F32)
    own_ids = ids[...]
    targets = assign[...]
    spots = lax.broadcasted_iota(jnp.int32, (1, 32), 1)
    for t in range(2):
        mark = jnp.zeros((32, 128), F32)
        for j in range(8):
            mark = mark + jnp.where(lane32 == own_ids[t : t + 1, j : j + 1] + 16, 0.125, 0.0)
        target = jnp.sum(
            jnp.where(spots == 2 * s + t, targets.astype(F32), 0.0), axis=1, keepdims=True
        )
        mark = mark + jnp.where(lane32 == 32, target * 0.125, 0.0)
        keep = jnp.ones((1, 1), F32) if t == 0 else accept[...].astype(F32)
        mark = mark + jnp.where(lane32 == 33, keep * 0.125, 0.0)
        facts = jnp.where(row32 == t, mark, facts)

    v_slot = slots(16)
    loads[2].wait()
    for r in (8, 10, 9, 11, 4, 12, 5, 13, 6, 14, 7, 15, 2, 3, 1, 0):
        owner = (s + r) % 16
        stats = facts
        halves = []
        for j in range(2):
            head = owner * 2 + j
            mine = [obuf[n, pl.ds(head, 32, stride=32), :] for n in range(5)]
            latent = jnp.concatenate(mine[:4], axis=1).astype(BF16)
            halves.append(mm(latent, wuv[head]).astype(BF16))
            level = mine[4]
            high = level.astype(BF16).astype(F32)
            middle = (level - high).astype(BF16).astype(F32)
            low = level - high - middle
            stats = jnp.where(lane32 == j * 64, high, stats)
            stats = jnp.where(lane32 == j * 64 + 1, middle, stats)
            stats = jnp.where(lane32 == j * 64 + 2, low, stats)
        message = jnp.concatenate(halves + [stats.astype(BF16)], axis=1)
        if r == 0:
            vrecv[s] = message
        else:
            vsend[r] = message
            send(vsend.at[r], vrecv.at[s], v_slot + s, member(owner))
    for r in range(1, 16):
        source = (s + r) % 16
        arrived(vrecv.at[source], v_slot + source)

    lane3 = lax.broadcasted_iota(jnp.int32, (16, 32, 128), 2)
    got = vrecv[:, :, pl.ds(256, 128)].astype(F32)
    values = []
    for j in range(2):
        inside = (lane3 >= j * 64) & (lane3 < j * 64 + 3)
        level = jnp.sum(jnp.where(inside, got, 0.0), axis=2, keepdims=True)
        share = jnp.exp2(level - jnp.max(level, axis=0, keepdims=True))
        total = jnp.sum(share, axis=0)
        heard = vrecv[:, :, pl.ds(j * 128, 128)].astype(F32)
        values.append(jnp.sum(heard * share, axis=0) / total)
    values = jnp.concatenate(values, axis=1).astype(BF16)

    pick_row = lax.broadcasted_iota(jnp.int32, (16, 128), 0)
    pick_lane = lax.broadcasted_iota(jnp.int32, (16, 128), 1)
    pick = (pick_lane == (pick_row >> 1) * 16 + (pick_row & 1)).astype(BF16)
    told = vrecv[pl.ds(k * 8, 8), pl.ds(0, 16), pl.ds(256, 128)].reshape(128, 128)
    facts = mm(pick, told)
    facts = jnp.where((pick_lane >= 16) & (pick_lane < 34), facts, 0.0)
    keep = jnp.sum(jnp.where(pick_lane == 33, facts, 0.0), axis=1, keepdims=True) * 8.0

    a_slot = slots(16)
    loads[3].wait()
    row_wide = lax.broadcasted_iota(jnp.int32, (32, COLS), 0)
    for dy in (2, 1, 3, 0):
        for dz in (1, 0):
            c = ((y + dy) % 4) * 2 + (zl + dz) % 2
            columns = pl.ds(pl.multiple_of(c * COLS, 128), COLS)
            part = mm(values, wout[:, columns])
            rest = residual[:, columns].astype(F32)
            part = part + jnp.where(
                row_wide == 2 * s,
                rest[0:1, :],
                jnp.where(row_wide == 2 * s + 1, rest[1:2, :], 0.0),
            )
            part = part.astype(BF16)
            n = (dy * 2 + dz) * 2
            asend[n] = part[:16]
            asend[n + 1] = part[16:]
            far = (dy, dz) != (0, 0)
            if far:
                for kk in range(2):
                    send(asend.at[n + kk], arecv.at[s], a_slot + s, member(c * 2 + kk))
            else:
                send(asend.at[n + 1 - k], arecv.at[s], a_slot + s, other)
                arecv[s] = asend[n + k]
    for r in range(1, 16):
        source = (s + r) % 16
        arrived(arecv.at[source], a_slot + source)
    hidden = jnp.sum(arecv[...].astype(F32), axis=0).astype(BF16).astype(F32)

    h_slot = slots(1)
    hbuf[k] = (hidden * keep).astype(BF16)
    send(hbuf.at[k], hbuf.at[k], h_slot, other)

    loads[4].wait()
    block = (hidden * gain[:, pl.ds(first_column, COLS)].astype(F32)).astype(BF16)
    squares = jnp.sum(hidden * hidden, axis=1, keepdims=True)
    squares_high = squares.astype(BF16).astype(F32)
    logits = nt(block, rpad[...])
    logits_high = logits.astype(BF16).astype(F32)
    note = logits_high + pltpu.roll(logits - logits_high, 16, 1) + pltpu.roll(facts, 32, 1)
    note = note + jnp.where(pick_lane == 32, squares_high, 0.0)
    note = note + jnp.where(pick_lane == 33, squares - squares_high, 0.0)
    tail = jnp.concatenate([block[:, 768:], note.astype(BF16)], axis=1)
    gathered = (xa, xb, xc)
    for buf, (w, _, order), piece in zip(
        gathered, PIECES, (block[:, :384], block[:, 384:768], tail)
    ):
        c1, c2, c3 = (at[axis] for axis in order)
        buf[k, c3, c2, c1] = piece

    plan = []
    for buf, (w, _, order) in zip(gathered, PIECES):
        plan.append((buf, order, tuple(at[axis] for axis in order), slots(3), slots(3), slots(6), slots(7)))
    for buf, order, (c1, c2, c3), s1, s2, s3, s4 in plan:
        mine = buf.at[k, c3, c2, c1]
        for o in (2, 1, 3):
            send(mine, mine, s1 + o - 1, peer(order[0], o))
    for buf, order, (c1, c2, c3), s1, s2, s3, s4 in plan:
        for o in (1, 3, 2):
            arrived(buf.at[k, c3, c2, (c1 + 4 - o) % 4], s1 + o - 1)
        mine = buf.at[k, c3, c2]
        for o in (2, 1, 3):
            send(mine, mine, s2 + o - 1, peer(order[1], o))

    def half(buf, plane, c3, h):
        return buf.at[plane, c3, pl.ds(2 * h, 2)]

    for buf, order, (c1, c2, c3), s1, s2, s3, s4 in plan:
        for o in (1, 3, 2):
            arrived(buf.at[k, c3, (c2 + 4 - o) % 4], s2 + o - 1)
        for h, o in ((0, 1), (1, 3), (1, 1), (0, 3)):
            mine = half(buf, k, c3, h)
            send(mine, mine, s3 + (0 if o == 1 else 2) + h, peer(order[2], o))
        send(buf.at[k, c3], buf.at[k, c3], s4 + 6, other)
    for step in range(3):
        for buf, order, (c1, c2, c3), s1, s2, s3, s4 in plan:
            left, right, far = (c3 + 3) % 4, (c3 + 1) % 4, (c3 + 2) % 4
            for n, c, h, onward in (
                ((0, left, 0, 1), (3, right, 1, 3)),
                ((1, left, 1, 0), (2, right, 0, 0)),
                ((4, far, 0, 0), (5, far, 1, 0)),
            )[step]:
                view = half(buf, k, c, h)
                arrived(view, s3 + n)
                if onward:
                    send(view, view, s3 + 4 + h, peer(order[2], onward))
                send(view, view, s4 + n, other)
    for buf, order, (c1, c2, c3), s1, s2, s3, s4 in plan:
        left, right, far = (c3 + 3) % 4, (c3 + 1) % 4, (c3 + 2) % 4
        arrived(buf.at[1 - k, c3], s4 + 6)
        for n, c, h in (
            (0, left, 0), (3, right, 1), (1, left, 1), (2, right, 0), (4, far, 0), (5, far, 1)
        ):
            arrived(half(buf, 1 - k, c, h), s4 + n)

    def rows_of(buf, order, yy, zz, columns):
        blocks = []
        for kk in range(2):
            for hh in range(2):
                for xx in range(4):
                    c = {"x": xx, "y": yy, "z": hh * 2 + zz}
                    c1, c2, c3 = (c[axis] for axis in order)
                    blocks.append(buf[kk, c3, c2, c1, :, columns])
        return jnp.concatenate(blocks, axis=0)

    note = jnp.zeros((256, 128), F32)
    gate_part = jnp.zeros((256, 256), F32)
    up_part = jnp.zeros((256, 256), F32)
    loads[5].wait()
    loads[6].wait()
    for yy in range(4):
        for zz in range(2):
            c = yy * 2 + zz
            tokens = jnp.concatenate(
                [
                    rows_of(xa, "xzy", yy, zz, pl.ds(0, 384)),
                    rows_of(xb, "yxz", yy, zz, pl.ds(0, 384)),
                    rows_of(xc, "zyx", yy, zz, pl.ds(0, 128)),
                ],
                axis=1,
            )
            note = note + rows_of(xc, "zyx", yy, zz, pl.ds(128, 128)).astype(F32)
            gate_part = gate_part + mm(tokens, wgate[pl.ds(c * COLS, COLS), :])
            up_part = up_part + mm(tokens, wup[pl.ds(c * COLS, COLS), :])

    lane = lax.broadcasted_iota(jnp.int32, (256, 128), 1)
    row = lax.broadcasted_iota(jnp.int32, (256, 128), 0)

    def column_sum(inside):
        return jnp.sum(jnp.where(inside, note, 0.0), axis=1, keepdims=True)

    model_width = 8 * COLS
    scale = lax.rsqrt(column_sum((lane == 32) | (lane == 33)) / model_width + norm_eps)
    logits = (note + pltpu.roll(note, 112, 1)) * scale
    chosen = jnp.where(lane < 16, jax.nn.sigmoid(logits) * pltpu.roll(note, 80, 1), 0.0)
    expert = (p * 16 + s) // 8
    gate = jnp.sum(jnp.where(lane == expert, chosen, 0.0), axis=1, keepdims=True)
    gate = gate / jnp.sum(chosen, axis=1, keepdims=True) * route_scale
    gate = gate * column_sum(lane == 65)
    act = jax.nn.silu(gate_part * scale) * (up_part * scale) * gate
    target = jnp.broadcast_to(column_sum(lane == 64), (256, 128)).astype(jnp.int32)
    place = ((target >> 1) & 1) * 128 + (row & 112) + (target >> 2) * 2 + (target & 1)
    place = jnp.transpose(place.astype(F32))[0:1, :]
    move = (lax.broadcasted_iota(jnp.int32, (256, 256), 0).astype(F32) == place).astype(BF16)
    act = mm(move, act.astype(BF16)).astype(BF16)

    loads[7].wait()
    partial = (pa, pb, pc)
    for yy in range(4):
        for zz in range(2):
            c = yy * 2 + zz
            part = mm(act, wdown[:, pl.ds(c * COLS, COLS)]).astype(BF16)
            start = 0
            for buf, (_, w, order) in zip(partial, PIECES):
                for kk in range(2):
                    for hh in range(2):
                        for xx in range(4):
                            at_block = {"x": xx, "y": yy, "z": hh * 2 + zz}
                            c1, c2, c3 = (at_block[axis] for axis in order)
                            first = ((kk * 2 + hh) * 4 + xx) * 16
                            buf[kk, c3, c2, c1] = part[first : first + 16, start : start + w]
                start += w

    plan = []
    for n, (_, w, order) in enumerate(PIECES):
        bufs = (partial[n], (r0a, r0b, r0c)[n], (r1a, r1b, r1c)[n])
        bufs += ((r2a, r2b, r2c)[n], (r3a, r3b, r3c)[n])
        plan.append((bufs, order, tuple(at[axis] for axis in order), slots(1), slots(6), slots(3), slots(3)))

    def add_to(ref, *terms):
        total = ref[...].astype(F32)
        for term in terms:
            total = total + term[...].astype(F32)
        ref[...] = total.astype(BF16)

    for (part, r0, r1, r2, r3), order, cs, s0, s1, s2, s3 in plan:
        send(part.at[1 - k], r0, s0, other)
    for (part, r0, r1, r2, r3), order, (c1, c2, c3), s0, s1, s2, s3 in plan:
        left, right, far = (c3 + 3) % 4, (c3 + 1) % 4, (c3 + 2) % 4
        arrived(r0, s0)
        for c in (far, right, left, c3):
            add_to(part.at[k, c], r0.at[c])
        to_right, to_left = peer(order[2], 1), peer(order[2], 3)
        send(half(part, k, far, 0), r1.at[0], s1, to_right)
        send(half(part, k, far, 1), r1.at[1], s1 + 1, to_left)
        send(half(part, k, right, 1), r1.at[2], s1 + 2, to_right)
        send(half(part, k, left, 0), r1.at[3], s1 + 3, to_left)
    for (part, r0, r1, r2, r3), order, (c1, c2, c3), s0, s1, s2, s3 in plan:
        left, right = (c3 + 3) % 4, (c3 + 1) % 4
        arrived(r1.at[0], s1)
        add_to(half(part, k, right, 0), r1.at[0])
        send(half(part, k, right, 0), r1.at[4], s1 + 4, peer(order[2], 1))
        arrived(r1.at[1], s1 + 1)
        add_to(half(part, k, left, 1), r1.at[1])
        send(half(part, k, left, 1), r1.at[5], s1 + 5, peer(order[2], 3))
    for (part, r0, r1, r2, r3), order, (c1, c2, c3), s0, s1, s2, s3 in plan:
        for n in (2, 3, 4, 5):
            arrived(r1.at[n], s1 + n)
        add_to(half(part, k, c3, 0), r1.at[3], r1.at[4])
        add_to(half(part, k, c3, 1), r1.at[2], r1.at[5])
        for o in (2, 1, 3):
            send(part.at[k, c3, (c2 + o) % 4], r2.at[o - 1], s2 + o - 1, peer(order[1], o))
    for (part, r0, r1, r2, r3), order, (c1, c2, c3), s0, s1, s2, s3 in plan:
        for o in (1, 2, 3):
            arrived(r2.at[o - 1], s2 + o - 1)
        add_to(part.at[k, c3, c2], r2.at[0], r2.at[1], r2.at[2])
        for o in (2, 1, 3):
            send(part.at[k, c3, c2, (c1 + o) % 4], r3.at[o - 1], s3 + o - 1, peer(order[0], o))
    sums = []
    for (part, r0, r1, r2, r3), order, (c1, c2, c3), s0, s1, s2, s3 in plan:
        for o in (1, 2, 3):
            arrived(r3.at[o - 1], s3 + o - 1)
        sums.append(part[k, c3, c2, c1].astype(F32) + jnp.sum(r3[...].astype(F32), axis=0))

    arrived(hbuf.at[1 - k], h_slot)
    i = lax.broadcasted_iota(jnp.int32, (16, 32), 0)
    move = ((i >> 1) * 4 + k * 2 + (i & 1) == targets).astype(BF16)
    final = jnp.concatenate(sums, axis=1) + mm(move, hbuf[...].reshape(32, COLS))
    for j in range(7):
        f1[j] = final[:, j * 128 : (j + 1) * 128]

    f2[...] = jnp.zeros_like(f2)
    for t in range(2):
        for j in range(7):
            f2[pl.ds(t * 7 + j, 8, stride=16), :] = f1[j, pl.ds(t, 8, stride=2), :]
    fsend[...] = f2[...].reshape(8, 16, 128).astype(BF16)
    f_slot = slots(8)
    for r in range(1, 8):
        c = (chip + r) % 8
        send(fsend.at[c], frecv.at[chip], f_slot + chip, member(c * 2 + k))
    frecv[chip] = fsend[chip]
    for r in range(1, 8):
        c = (chip + r) % 8
        arrived(frecv.at[c], f_slot + c)
    result[...] = frecv[...]
    links.finish()


def local(
    queries,
    new_keys,
    cache,
    residual,
    w_uv,
    w_out,
    norm_gain,
    router,
    expert_ids,
    w_gate,
    w_up,
    w_down,
    accept,
    assign,
):
    positions = cache.shape[1]
    whole = pl.BlockSpec(memory_space=pltpu.VMEM)
    left = pl.BlockSpec(memory_space=pl.ANY)
    scratch = [
        pltpu.VMEM((576, positions), BF16),
        pltpu.VMEM((32, 512, 128), BF16),
        pltpu.VMEM((256, 7168), BF16),
        pltpu.VMEM((7168, 256), BF16),
        pltpu.VMEM((7168, 256), BF16),
        pltpu.VMEM((256, 7168), BF16),
        pltpu.VMEM((128, COLS), BF16),
        pltpu.VMEM((16, 64, 576), BF16),
        pltpu.VMEM((128, 576), BF16),
        pltpu.VMEM((5, 1024, 128), F32),
        pltpu.VMEM((16, 32, 384), BF16),
        pltpu.VMEM((16, 32, 384), BF16),
        pltpu.VMEM((16, 16, COLS), BF16),
        pltpu.VMEM((16, 16, COLS), BF16),
        pltpu.VMEM((2, 16, COLS), BF16),
    ]
    scratch += [pltpu.VMEM((2, 4, 4, 4, 16, w), BF16) for w, _, _ in PIECES]
    scratch += [pltpu.VMEM((2, 4, 4, 4, 16, w), BF16) for _, w, _ in PIECES]
    scratch += [pltpu.VMEM((4, 4, 4, 16, w), BF16) for _, w, _ in PIECES]
    scratch += [pltpu.VMEM((6, 2, 4, 16, w), BF16) for _, w, _ in PIECES]
    scratch += [pltpu.VMEM((3, 4, 16, w), BF16) for _, w, _ in PIECES]
    scratch += [pltpu.VMEM((3, 16, w), BF16) for _, w, _ in PIECES]
    scratch += [
        pltpu.VMEM((7, 16, 128), F32),
        pltpu.VMEM((128, 128), F32),
        pltpu.VMEM((8, 16, 128), BF16),
        pltpu.VMEM((8, 16, 128), BF16),
        pltpu.SemaphoreType.DMA((8,)),
        pltpu.SemaphoreType.DMA((192,)),
        pltpu.SemaphoreType.DMA((192,)),
    ]
    rows = pl.pallas_call(
        kernel,
        out_shape=jax.ShapeDtypeStruct((8, 16, 128), BF16),
        in_specs=[left] * 8 + [whole] * 6,
        out_specs=whole,
        scratch_shapes=scratch,
        compiler_params=pltpu.CompilerParams(
            collective_id=0, has_side_effects=True, vmem_limit_bytes=60 * 1024 * 1024
        ),
        name="layer",
    )(
        queries.reshape(64, 576),
        cache[0].T,
        w_uv,
        w_out,
        router.T,
        w_gate[0],
        w_up[0],
        w_down[0],
        new_keys,
        residual,
        norm_gain.reshape(1, 7168),
        expert_ids,
        accept,
        assign,
    )
    rows = rows[:, :14].reshape(8, 2, 7, 128).transpose(1, 0, 2, 3)
    return rows.reshape(2, 7168)


def solution(mesh):
    placed = (
        P(("prompt", "sample"), None, None),
        P(("prompt", "sample"), None),
        P("prompt", "sample", None),
        P(("prompt", "sample"), None),
        P(),
        P("sample", None),
        P(),
        P(),
        P(("prompt", "sample"), None),
        P(("prompt", "sample"), None, None),
        P(("prompt", "sample"), None, None),
        P(("prompt", "sample"), None, None),
        P("prompt", "sample"),
        P("prompt", None),
    )
    return jax.shard_map(
        local, mesh=mesh, in_specs=placed, out_specs=P(("prompt", "sample"), None), check_vma=False
    )
```

```python
import functools
import jax
import jax.numpy as jnp
from jax import lax
from jax.experimental import pallas as pl
from jax.experimental.pallas import tpu as pltpu
from jax.sharding import PartitionSpec as P

MESH = pl.DeviceIdType.MESH
F32 = jnp.float32
BF16 = jnp.bfloat16
score_scale = 192.0 ** (-0.5)
log2e = 1.4426950408889634
route_scale = 2.827
norm_eps = 1e-06

COLS = 896
PIECES = ((384, 384, "xzy"), (384, 256, "yxz"), (256, 256, "zyx"))


def nt(a, b):
    return lax.dot_general(a, b, (((1,), (1,)), ((), ())), preferred_element_type=F32)


def mm(a, b):
    return jnp.dot(a, b, preferred_element_type=F32)


class Links:
    def __init__(self, send_sem, recv_sem, anyone):
        self.send_sem, self.recv_sem, self.anyone = send_sem, recv_sem, anyone
        self.sent, self.taken = [], 0

    def slots(self, n=1):
        self.taken += n
        return self.taken - n

    def send(self, src, dst, slot, device):
        copy = pltpu.make_async_remote_copy(
            src_ref=src,
            dst_ref=dst,
            send_sem=self.send_sem.at[len(self.sent)],
            recv_sem=self.recv_sem.at[slot],
            device_id=device,
            device_id_type=MESH,
        )
        copy.start()
        self.sent.append(copy)

    def arrived(self, dst, slot):
        pltpu.make_async_remote_copy(
            src_ref=dst,
            dst_ref=dst,
            send_sem=self.send_sem.at[0],
            recv_sem=self.recv_sem.at[slot],
            device_id=self.anyone,
            device_id_type=MESH,
        ).wait_recv()

    def finish(self):
        for copy in self.sent:
            copy.wait_send()


def kernel(
    q_in,
    cache_in,
    uv_in,
    out_in,
    router_in,
    gate_in,
    up_in,
    down_in,
    new_keys,
    residual,
    gain,
    ids,
    accept,
    assign,
    result,
    kc,
    wuv,
    wout,
    wgate,
    wup,
    wdown,
    rpad,
    qbuf,
    kn,
    obuf,
    vsend,
    vrecv,
    asend,
    arecv,
    hbuf,
    xa,
    xb,
    xc,
    pa,
    pb,
    pc,
    r1a,
    r1b,
    r1c,
    r2a,
    r2b,
    r2c,
    r3a,
    r3b,
    r3c,
    f1,
    f2,
    fsend,
    frecv,
    gf,
    load_sem,
    send_sem,
    recv_sem,
):
    p = lax.axis_index("prompt")
    s = lax.axis_index("sample")
    x, zh = p // 2, p % 2
    y, zl, k = s // 4, (s // 2) % 2, s % 2
    z = zh * 2 + zl
    chip = y * 2 + zl
    at = {"x": x, "y": y, "z": z}

    def device(x, y, z, k):
        return (x * 2 + z // 2, y * 4 + (z % 2) * 2 + k)

    def peer(axis, step):
        there = dict(at)
        there[axis] = (at[axis] + step) % 4
        return device(there["x"], there["y"], there["z"], k)

    def member(t):
        return (p, t)

    other = (p, y * 4 + zl * 2 + (1 - k))
    across = (p, y * 4 + (1 - zl) * 2 + k)

    first_column = pl.multiple_of(chip * COLS, 128)
    own_heads = pl.ds(pl.multiple_of(k * 16, 16), 16)
    own_units = pl.ds(pl.multiple_of(k * 256, 256), 256)
    loads = [
        pltpu.make_async_copy(src, dst, load_sem.at[n])
        for n, (src, dst) in enumerate(
            (
                (q_in.at[:, own_heads], qbuf.at[s]),
                (cache_in, kc.at[k]),
                (uv_in.at[own_heads], wuv),
                (out_in, wout),
                (router_in.at[:, pl.ds(first_column, COLS)], rpad.at[pl.ds(0, 16)]),
                (gate_in, wgate.at[k]),
                (up_in, wup.at[k]),
                (down_in, wdown.at[own_units]),
            )
        )
    ]
    for n in (0, 1, 2):
        loads[n].start()

    barrier = pltpu.get_barrier_semaphore()
    partners = [member((s + r) % 16) for r in range(1, 16)]
    partners += [peer("x", r) for r in (1, 2, 3)]
    partners += [device(x, y, (1 - zh) * 2 + r, k) for r in (0, 1)]
    for there in partners:
        pl.semaphore_signal(barrier, inc=1, device_id=there, device_id_type=MESH)
    pl.semaphore_wait(barrier, len(partners))

    links = Links(send_sem, recv_sem, other)
    send, arrived, slots = links.send, links.arrived, links.slots

    q_slot = slots(16)
    k_slot = slots(2)
    for dy in (0, 1, 3, 2):
        for dz in (0, 1):
            for dk in (1, 0):
                if (dy, dz, dk) == (0, 0, 0):
                    continue
                kk = (k + dk) % 2
                t = ((y + dy) % 4) * 4 + ((zl + dz) % 2) * 2 + kk
                heads = pl.ds(pl.multiple_of(kk * 16, 16), 16)
                send(q_in.at[:, heads], qbuf.at[s], q_slot + s, member(t))
        if dy == 0:
            send(cache_in, kc.at[k], k_slot, other)

    fresh = new_keys[...].astype(F32)
    row = lax.broadcasted_iota(jnp.int32, (16, 576), 0)
    kn[own_heads] = jnp.where(
        row == 0, fresh[0:1, :], jnp.where(row == 1, fresh[1:2, :], 0.0)
    ).astype(BF16)
    send(kn.at[own_heads], kn.at[own_heads], k_slot + 1, other)
    kn[pl.ds(32, 96)] = jnp.zeros((96, 576), BF16)
    rpad[pl.ds(16, 112)] = jnp.zeros((112, COLS), BF16)

    to_log2 = score_scale * log2e

    def attend(ya, yb, own):
        for yy in (ya, yb):
            for n in range(4):
                t = yy * 4 + n
                if own and yy is y:
                    t = y * 4 + (zl * 2 + k + n) % 4
                    if n == 0:
                        continue
                arrived(qbuf.at[t], q_slot + t)
        q = jnp.concatenate(
            [qbuf[pl.ds(yy * 4, 4)].reshape(128, 576) for yy in (ya, yb)], axis=0
        )
        scores = [mm(q, kc[n]) * to_log2 for n in range(2)]
        peaks = [jnp.max(part, axis=1, keepdims=True) for part in scores]
        peak = jnp.maximum(peaks[0], peaks[1])
        if own:
            row = lax.broadcasted_iota(jnp.int32, (256, 128), 0) - zl * 64
            column = lax.broadcasted_iota(jnp.int32, (256, 128), 1)
            seen = (
                (row >= 0)
                & (row < 64)
                & ((column >> 4) == (row >> 5))
                & ((column & 15) <= ((row >> 4) & 1))
            )
            own_scores = jnp.where(seen, nt(q, kn[...]) * to_log2, -jnp.inf)
            peak = jnp.maximum(peak, jnp.max(own_scores, axis=1, keepdims=True))
        denom = jnp.zeros((256, 1), F32)
        latent = jnp.zeros((256, 512), F32)
        for n in range(2):
            weights = jnp.exp2(scores[n] - peak)
            denom = denom + jnp.sum(weights, axis=1, keepdims=True)
            latent = latent + nt(weights.astype(BF16), kc[n, pl.ds(0, 512), :])
        if own:
            own_weights = jnp.exp2(own_scores - peak)
            denom = denom + jnp.sum(own_weights, axis=1, keepdims=True)
            latent = latent + mm(own_weights.astype(BF16), kn[:, pl.ds(0, 512)])
        latent = latent / denom
        level = jnp.broadcast_to(peak + jnp.log2(denom), (256, 128))
        for i, yy in enumerate((ya, yb)):
            at_rows = pl.ds(pl.multiple_of(yy * 128, 128), 128)
            for n in range(4):
                obuf[n, at_rows, :] = latent[i * 128 : i * 128 + 128, n * 128 : n * 128 + 128]
            obuf[4, at_rows, :] = level[i * 128 : i * 128 + 128]

    loads[0].wait()
    loads[1].wait()
    arrived(kn.at[pl.ds(pl.multiple_of(16 - k * 16, 16), 16)], k_slot + 1)
    arrived(kc.at[1 - k], k_slot)
    for n in (3, 4, 5, 6, 7):
        loads[n].start()
    w_slot = slots(3)
    send(gate_in, wgate.at[k], w_slot, other)
    send(up_in, wup.at[k], w_slot + 1, other)
    send(down_in, wdown.at[own_units], w_slot + 2, other)
    attend(y, (y + 1) % 4, True)
    attend((y + 3) % 4, (y + 2) % 4, False)

    lane32 = lax.broadcasted_iota(jnp.int32, (32, 128), 1)
    v_slot = slots(8)
    own_share = (s // 8) == k
    loads[2].wait()
    own_send = None
    for r in (4, 5, 3, 6, 2, 7, 1, 0):
        local_owner = (s + r) % 8
        owner = k * 8 + local_owner
        stats = jnp.zeros((32, 128), F32)
        halves = []
        for j in range(2):
            head = local_owner * 2 + j
            mine = [obuf[n, pl.ds(head, 32, stride=16), :] for n in range(5)]
            latent = jnp.concatenate(mine[:4], axis=1).astype(BF16)
            halves.append(mm(latent, wuv[head]).astype(BF16))
            level = mine[4]
            high = level.astype(BF16).astype(F32)
            middle = (level - high).astype(BF16).astype(F32)
            low = level - high - middle
            stats = jnp.where(lane32 == j * 64, high, stats)
            stats = jnp.where(lane32 == j * 64 + 1, middle, stats)
            stats = jnp.where(lane32 == j * 64 + 2, low, stats)
        vsend[r] = jnp.concatenate(halves + [stats.astype(BF16)], axis=1)
        if r:
            send(vsend.at[r], vrecv.at[chip], v_slot + chip, member(owner))
        else:
            own_send = pltpu.make_async_remote_copy(
                src_ref=vsend.at[r],
                dst_ref=vrecv.at[chip],
                send_sem=load_sem.at[8],
                recv_sem=recv_sem.at[v_slot + chip],
                device_id=member(owner),
                device_id_type=MESH,
            )

            @pl.when(own_share)
            def _():
                vrecv[chip] = vsend[0]

            @pl.when(jnp.logical_not(own_share))
            def _():
                own_send.start()

    row32 = lax.broadcasted_iota(jnp.int32, (32, 128), 0)
    own_ids = ids[...]
    targets = assign[...]
    places = ((targets >> 1) & 1) * 16 + (targets >> 2) * 2 + (targets & 1)
    move = (lax.broadcasted_iota(jnp.int32, (32, 32), 0) == places).astype(BF16)
    spots = lax.broadcasted_iota(jnp.int32, (1, 32), 1)

    facts = jnp.zeros((32, 128), F32)
    own_places = []
    for t in range(2):
        mark = jnp.zeros((32, 128), F32)
        for j in range(8):
            mark = mark + jnp.where(lane32 == own_ids[t : t + 1, j : j + 1] + 48, 0.125, 0.0)
        keep = jnp.ones((1, 1), F32) if t == 0 else accept[...].astype(F32)
        mark = mark + jnp.where(lane32 == 65, keep, 0.0)
        place = jnp.sum(jnp.where(spots == 2 * s + t, places, 0), axis=1, keepdims=True)
        own_places.append(place)
        facts = jnp.where(row32 == place, mark, facts)
    facts = facts.astype(BF16)

    for r in range(1, 8):
        c = (chip + r) % 8
        arrived(vrecv.at[c], v_slot + c)

    @pl.when(jnp.logical_not(own_share))
    def _():
        arrived(vrecv.at[chip], v_slot + chip)
        own_send.wait_send()

    lane3 = lax.broadcasted_iota(jnp.int32, (8, 32, 128), 2)
    got = vrecv[:, :, pl.ds(256, 128)].astype(F32)
    values = []
    for j in range(2):
        inside = (lane3 >= j * 64) & (lane3 < j * 64 + 3)
        level = jnp.sum(jnp.where(inside, got, 0.0), axis=2, keepdims=True)
        share = jnp.exp2(level - jnp.max(level, axis=0, keepdims=True))
        total = jnp.sum(share, axis=0)
        heard = vrecv[:, :, pl.ds(j * 128, 128)].astype(F32)
        values.append(jnp.sum(heard * share, axis=0) / total)
    values = jnp.concatenate(values, axis=1).astype(BF16)
    values = mm(move, values).astype(BF16)

    a_slot = slots(16)
    loads[3].wait()
    row_wide = lax.broadcasted_iota(jnp.int32, (32, COLS), 0)
    for dy in (2, 1, 3, 0):
        for dz in (1, 0):
            c = ((y + dy) % 4) * 2 + (zl + dz) % 2
            columns = pl.ds(pl.multiple_of(c * COLS, 128), COLS)
            part = mm(values, wout[:, columns])
            rest = residual[:, columns].astype(F32)
            part = part + jnp.where(
                row_wide == own_places[0],
                rest[0:1, :],
                jnp.where(row_wide == own_places[1], rest[1:2, :], 0.0),
            )
            part = jnp.concatenate([part.astype(BF16), facts], axis=1)
            n = (dy * 2 + dz) * 2
            asend[n] = part[:16]
            asend[n + 1] = part[16:]
            far = (dy, dz) != (0, 0)
            if far:
                for kk in range(2):
                    send(asend.at[n + kk], arecv.at[s], a_slot + s, member(c * 2 + kk))
            else:
                send(asend.at[n + 1 - k], arecv.at[s], a_slot + s, other)
                arecv[s] = asend[n + k]
    for r in range(1, 16):
        source = (s + r) % 16
        arrived(arecv.at[source], a_slot + source)
    total = jnp.sum(arecv[...].astype(F32), axis=0)
    hidden = total[:, :COLS].astype(BF16).astype(F32)
    facts = total[:, COLS:]
    note_lane = lax.broadcasted_iota(jnp.int32, (16, 128), 1)
    keep = jnp.sum(jnp.where(note_lane == 65, facts, 0.0), axis=1, keepdims=True)

    hbuf[...] = hidden

    loads[4].wait()
    gf[...] = gain[...].astype(F32)
    own_gain = jnp.concatenate([gf[pl.ds(chip * 7 + j, 1), :] for j in range(7)], axis=1)
    block = (hidden * own_gain).astype(BF16)
    squares = jnp.sum(hidden * hidden, axis=1, keepdims=True)
    squares_high = squares.astype(BF16).astype(F32)
    logits = nt(block, rpad[...])
    logits_high = logits.astype(BF16).astype(F32)
    note = logits_high + pltpu.roll(logits - logits_high, 16, 1) + facts
    note = note + jnp.where(note_lane == 32, squares_high, 0.0)
    note = note + jnp.where(note_lane == 33, squares - squares_high, 0.0)
    tail = jnp.concatenate([block[:, 768:], note.astype(BF16)], axis=1)
    gathered = (xa, xb, xc)
    for buf, (w, _, order), piece in zip(
        gathered, PIECES, (block[:, :384], block[:, 384:768], tail)
    ):
        c1, c2, c3 = (at[axis] for axis in order)
        buf[c3, c2, c1] = piece

    plan = []
    for buf, (w, _, order) in zip(gathered, PIECES):
        plan.append((buf, order, tuple(at[axis] for axis in order), slots(3), slots(3), slots(6)))
    for o in (2, 1, 3):
        for buf, order, (c1, c2, c3), s1, s2, s3 in plan:
            mine = buf.at[c3, c2, c1]
            send(mine, mine, s1 + o - 1, peer(order[0], o))
    for buf, order, (c1, c2, c3), s1, s2, s3 in plan:
        for o in (1, 3, 2):
            arrived(buf.at[c3, c2, (c1 + 4 - o) % 4], s1 + o - 1)
        mine = buf.at[c3, c2]
        for o in (2, 1, 3):
            send(mine, mine, s2 + o - 1, peer(order[1], o))
    for buf, order, (c1, c2, c3), s1, s2, s3 in plan:
        for o in (1, 3, 2):
            arrived(buf.at[c3, (c2 + 4 - o) % 4], s2 + o - 1)

    def half(buf, c3, h):
        return buf.at[c3, pl.ds(2 * h, 2)]

    for h, o in ((0, 1), (1, 3), (0, 3), (1, 1)):
        for buf, order, (c1, c2, c3), s1, s2, s3 in plan:
            mine = half(buf, c3, h)
            send(mine, mine, s3 + (0 if o == 1 else 2) + h, peer(order[2], o))

    def rows_of(n, yy, zz, columns):
        blocks = []
        for hh in range(2):
            for xx in range(4):
                c = {"x": xx, "y": yy, "z": hh * 2 + zz}
                c1, c2, c3 = (c[axis] for axis in PIECES[n][2])
                blocks.append(gathered[n][c3, c2, c1, :, columns])
        return jnp.concatenate(blocks, axis=0)

    parts = [[jnp.zeros((128, 256), F32) for _ in range(2)] for _ in range(2)]

    def multiply(n, yy, first, width):
        for zz in range(2):
            tokens = rows_of(n, yy, zz, pl.ds(0, width))
            at_rows = pl.ds(pl.multiple_of((yy * 2 + zz) * COLS + first, 128), width)
            for b in range(2):
                parts[b][0] = parts[b][0] + mm(tokens, wgate[b, at_rows, :])
                parts[b][1] = parts[b][1] + mm(tokens, wup[b, at_rows, :])

    loads[5].wait()
    loads[6].wait()
    arrived(wgate.at[1 - k], w_slot)
    arrived(wup.at[1 - k], w_slot + 1)
    multiply(0, y, 0, 384)
    for buf, order, (c1, c2, c3), s1, s2, s3 in plan:
        for c, h, n, o in (((c3 + 3) % 4, 0, 0, 1), ((c3 + 1) % 4, 1, 3, 3)):
            view = half(buf, c, h)
            arrived(view, s3 + n)
            send(view, view, s3 + 4 + h, peer(order[2], o))

    def rest(n, last):
        buf, order, (c1, c2, c3), s1, s2, s3 = plan[n]
        if last:
            arrived(half(buf, (c3 + 2) % 4, 0), s3 + 4)
            arrived(half(buf, (c3 + 2) % 4, 1), s3 + 5)
        else:
            arrived(half(buf, (c3 + 3) % 4, 1), s3 + 1)
            arrived(half(buf, (c3 + 1) % 4, 0), s3 + 2)

    rest(0, False)
    multiply(0, (y + 3) % 4, 0, 384)
    multiply(0, (y + 1) % 4, 0, 384)
    rest(0, True)
    multiply(0, (y + 2) % 4, 0, 384)
    rest(1, False)
    rest(1, True)
    for yy in range(4):
        multiply(1, yy, 384, 384)
    rest(2, False)
    rest(2, True)
    note = jnp.zeros((128, 128), F32)
    for yy in range(4):
        multiply(2, yy, 768, 128)
        for zz in range(2):
            note = note + rows_of(2, yy, zz, pl.ds(128, 128)).astype(F32)

    lane = lax.broadcasted_iota(jnp.int32, (128, 128), 1)

    def column_sum(inside):
        return jnp.sum(jnp.where(inside, note, 0.0), axis=1, keepdims=True)

    model_width = 8 * COLS
    scale = lax.rsqrt(column_sum((lane == 32) | (lane == 33)) / model_width + norm_eps)
    logits = (note + pltpu.roll(note, 112, 1)) * scale
    chosen = jnp.where(lane < 16, jax.nn.sigmoid(logits) * pltpu.roll(note, 80, 1), 0.0)
    expert = (p * 16 + s) // 8
    gate = jnp.sum(jnp.where(lane == expert, chosen, 0.0), axis=1, keepdims=True)
    gate = gate / jnp.sum(chosen, axis=1, keepdims=True) * route_scale
    act = [jax.nn.silu(g * scale) * (u * scale) * gate for g, u in parts]
    act = jnp.concatenate(act, axis=1).astype(BF16)

    loads[7].wait()
    arrived(wdown.at[pl.ds(pl.multiple_of(256 - k * 256, 256), 256)], w_slot + 2)
    partial = (pa, pb, pc)
    for yy in range(4):
        for zz in range(2):
            part = mm(act, wdown[:, pl.ds((yy * 2 + zz) * COLS, COLS)]).astype(BF16)
            start = 0
            for buf, (_, w, order) in zip(partial, PIECES):
                for hh in range(2):
                    for xx in range(4):
                        at_block = {"x": xx, "y": yy, "z": hh * 2 + zz}
                        c1, c2, c3 = (at_block[axis] for axis in order)
                        first = (hh * 4 + xx) * 16
                        buf[c3, c2, c1] = part[first : first + 16, start : start + w]
                start += w
    plan = []
    for n, (_, w, order) in enumerate(PIECES):
        bufs = (partial[n], (r1a, r1b, r1c)[n], (r2a, r2b, r2c)[n], (r3a, r3b, r3c)[n])
        plan.append((bufs, order, tuple(at[axis] for axis in order), slots(6), slots(3), slots(3)))

    def add_to(ref, *terms):
        total = ref[...].astype(F32)
        for term in terms:
            total = total + term[...].astype(F32)
        ref[...] = total.astype(BF16)

    for n, (step, h, o) in enumerate(((2, 0, 1), (2, 1, 3), (1, 1, 1), (3, 0, 3))):
        for (part, r1, r2, r3), order, (c1, c2, c3), s1, s2, s3 in plan:
            send(half(part, (c3 + step) % 4, h), r1.at[n], s1 + n, peer(order[2], o))
    for n, (step, h, o) in enumerate(((1, 0, 1), (3, 1, 3))):
        for (part, r1, r2, r3), order, (c1, c2, c3), s1, s2, s3 in plan:
            view = half(part, (c3 + step) % 4, h)
            arrived(r1.at[n], s1 + n)
            add_to(view, r1.at[n])
            send(view, r1.at[n + 4], s1 + n + 4, peer(order[2], o))
    for (part, r1, r2, r3), order, (c1, c2, c3), s1, s2, s3 in plan:
        for n in (2, 3, 4, 5):
            arrived(r1.at[n], s1 + n)
        add_to(half(part, c3, 0), r1.at[3], r1.at[4])
        add_to(half(part, c3, 1), r1.at[2], r1.at[5])
        for o in (2, 1, 3):
            send(part.at[c3, (c2 + o) % 4], r2.at[o - 1], s2 + o - 1, peer(order[1], o))
    for (part, r1, r2, r3), order, (c1, c2, c3), s1, s2, s3 in plan:
        for o in (1, 2, 3):
            arrived(r2.at[o - 1], s2 + o - 1)
        add_to(part.at[c3, c2], r2.at[0], r2.at[1], r2.at[2])
        for o in (2, 1, 3):
            send(part.at[c3, c2, (c1 + o) % 4], r3.at[o - 1], s3 + o - 1, peer(order[0], o))
    sums = []
    for (part, r1, r2, r3), order, (c1, c2, c3), s1, s2, s3 in plan:
        for o in (1, 2, 3):
            arrived(r3.at[o - 1], s3 + o - 1)
        sums.append(part[c3, c2, c1].astype(F32) + jnp.sum(r3[...].astype(F32), axis=0))
    final = (jnp.concatenate(sums, axis=1) + hbuf[...]) * keep
    for j in range(7):
        f1[j] = final[:, j * 128 : (j + 1) * 128]

    f2[...] = jnp.zeros_like(f2)
    for t in range(2):
        for j in range(7):
            f2[pl.ds(t * 7 + j, 8, stride=16), :] = f1[j, pl.ds(t, 8, stride=2), :]
    fsend[...] = f2[...].reshape(8, 16, 128).astype(BF16)
    f_slot = slots(8)
    for r in range(1, 8):
        c = (chip + r) % 8
        send(fsend.at[c], frecv.at[chip], f_slot + chip, member(c * 2 + k))
    frecv[chip] = fsend[chip]
    for r in range(1, 8):
        c = (chip + r) % 8
        arrived(frecv.at[c], f_slot + c)
    f2[...] = frecv[...].reshape(128, 128).astype(F32)
    rows = [f2[pl.ds(c * 16 + j, 2, stride=7), :] for c in range(8) for j in range(7)]
    result[...] = jnp.concatenate(rows, axis=1).astype(BF16)
    links.finish()


def local(
    queries,
    new_keys,
    cache,
    residual,
    w_uv,
    w_out,
    norm_gain,
    router,
    expert_ids,
    w_gate,
    w_up,
    w_down,
    accept,
    assign,
):
    positions = cache.shape[1]
    whole = pl.BlockSpec(memory_space=pltpu.VMEM)
    left = pl.BlockSpec(memory_space=pl.ANY)
    scratch = [
        pltpu.VMEM((2, 576, positions), BF16),
        pltpu.VMEM((16, 512, 128), BF16),
        pltpu.VMEM((256, 7168), BF16),
        pltpu.VMEM((2, 7168, 256), BF16),
        pltpu.VMEM((2, 7168, 256), BF16),
        pltpu.VMEM((512, 7168), BF16),
        pltpu.VMEM((128, COLS), BF16),
        pltpu.VMEM((16, 2, 16, 576), BF16),
        pltpu.VMEM((128, 576), BF16),
        pltpu.VMEM((5, 512, 128), F32),
        pltpu.VMEM((8, 32, 384), BF16),
        pltpu.VMEM((8, 32, 384), BF16),
        pltpu.VMEM((16, 16, COLS + 128), BF16),
        pltpu.VMEM((16, 16, COLS + 128), BF16),
        pltpu.VMEM((16, COLS), F32),
    ]
    scratch += [pltpu.VMEM((4, 4, 4, 16, w), BF16) for w, _, _ in PIECES]
    scratch += [pltpu.VMEM((4, 4, 4, 16, w), BF16) for _, w, _ in PIECES]
    scratch += [pltpu.VMEM((6, 2, 4, 16, w), BF16) for _, w, _ in PIECES]
    scratch += [pltpu.VMEM((3, 4, 16, w), BF16) for _, w, _ in PIECES]
    scratch += [pltpu.VMEM((3, 16, w), BF16) for _, w, _ in PIECES]
    scratch += [
        pltpu.VMEM((7, 16, 128), F32),
        pltpu.VMEM((128, 128), F32),
        pltpu.VMEM((8, 16, 128), BF16),
        pltpu.VMEM((8, 16, 128), BF16),
        pltpu.VMEM((56, 128), F32),
        pltpu.SemaphoreType.DMA((9,)),
        pltpu.SemaphoreType.DMA((192,)),
        pltpu.SemaphoreType.DMA((192,)),
    ]
    rows = pl.pallas_call(
        kernel,
        out_shape=jax.ShapeDtypeStruct((2, 7168), BF16),
        in_specs=[left] * 8 + [whole] * 6,
        out_specs=whole,
        scratch_shapes=scratch,
        compiler_params=pltpu.CompilerParams(
            collective_id=0, has_side_effects=True, vmem_limit_bytes=60 * 1024 * 1024
        ),
        name="layer",
    )(
        queries,
        cache[0].T,
        w_uv,
        w_out,
        router.T,
        w_gate[0],
        w_up[0],
        w_down[0],
        new_keys,
        residual,
        norm_gain.reshape(56, 128),
        expert_ids,
        accept,
        assign,
    )
    return rows


def solution(mesh):
    placed = (
        P(("prompt", "sample"), None, None),
        P(("prompt", "sample"), None),
        P("prompt", "sample", None),
        P(("prompt", "sample"), None),
        P(),
        P("sample", None),
        P(),
        P(),
        P(("prompt", "sample"), None),
        P(("prompt", "sample"), None, None),
        P(("prompt", "sample"), None, None),
        P(("prompt", "sample"), None, None),
        P("prompt", "sample"),
        P("prompt", None),
    )
    return jax.shard_map(
        local, mesh=mesh, in_specs=placed, out_specs=P(("prompt", "sample"), None), check_vma=False
    )
```

```python
import functools
import jax
import jax.numpy as jnp
from jax import lax
from jax.experimental import pallas as pl
from jax.experimental.pallas import tpu as pltpu
from jax.sharding import PartitionSpec as P

MESH = pl.DeviceIdType.MESH
F32 = jnp.float32
BF16 = jnp.bfloat16
score_scale = 192.0 ** (-0.5)
log2e = 1.4426950408889634
route_scale = 2.827
norm_eps = 1e-06

COLS = 896
PIECES = ((384, 384, "xzy"), (384, 256, "yxz"), (256, 256, "zyx"))


def nt(a, b):
    return lax.dot_general(a, b, (((1,), (1,)), ((), ())), preferred_element_type=F32)


def mm(a, b):
    return jnp.dot(a, b, preferred_element_type=F32)


class Links:
    def __init__(self, send_sem, recv_sem, anyone):
        self.send_sem, self.recv_sem, self.anyone = send_sem, recv_sem, anyone
        self.sent, self.taken = [], 0

    def slots(self, n=1):
        self.taken += n
        return self.taken - n

    def send(self, src, dst, slot, device):
        copy = pltpu.make_async_remote_copy(
            src_ref=src,
            dst_ref=dst,
            send_sem=self.send_sem.at[len(self.sent)],
            recv_sem=self.recv_sem.at[slot],
            device_id=device,
            device_id_type=MESH,
        )
        copy.start()
        self.sent.append(copy)

    def arrived(self, dst, slot):
        pltpu.make_async_remote_copy(
            src_ref=dst,
            dst_ref=dst,
            send_sem=self.send_sem.at[0],
            recv_sem=self.recv_sem.at[slot],
            device_id=self.anyone,
            device_id_type=MESH,
        ).wait_recv()

    def finish(self):
        for copy in self.sent:
            copy.wait_send()


def kernel(
    q_in,
    cache_in,
    uv_in,
    out_in,
    router_in,
    gate_in,
    up_in,
    down_in,
    new_keys,
    residual,
    gain,
    ids,
    accept,
    assign,
    result,
    kc,
    wuv,
    wout,
    wgate,
    wup,
    wdown,
    rpad,
    qbuf,
    kn,
    obuf,
    vsend,
    vrecv,
    asend,
    arecv,
    stage,
    xa,
    xb,
    xc,
    pa,
    pb,
    pc,
    r1a,
    r1b,
    r1c,
    r2a,
    r2b,
    r2c,
    f1,
    f2,
    fsend,
    frecv,
    gf,
    extra,
    load_sem,
    send_sem,
    recv_sem,
):
    p = lax.axis_index("prompt")
    s = lax.axis_index("sample")
    x, zh = p // 2, p % 2
    y, zl, k = s // 4, (s // 2) % 2, s % 2
    z = zh * 2 + zl
    chip = y * 2 + zl
    at = {"x": x, "y": y, "z": z}

    def device(x, y, z, k):
        return (x * 2 + z // 2, y * 4 + (z % 2) * 2 + k)

    def peer(axis, step):
        there = dict(at)
        there[axis] = (at[axis] + step) % 4
        return device(there["x"], there["y"], there["z"], k)

    def beside(order, o1, o2):
        there = dict(at)
        there[order[0]] = (at[order[0]] + o1) % 4
        there[order[1]] = (at[order[1]] + o2) % 4
        return device(there["x"], there["y"], there["z"], k)

    def member(t):
        return (p, t)

    other = (p, y * 4 + zl * 2 + (1 - k))
    across = (p, y * 4 + (1 - zl) * 2 + k)

    first_column = pl.multiple_of(chip * COLS, 128)
    own_heads = pl.ds(pl.multiple_of(k * 16, 16), 16)
    own_units = pl.ds(pl.multiple_of(k * 256, 256), 256)
    loads = [
        pltpu.make_async_copy(src, dst, load_sem.at[n])
        for n, (src, dst) in enumerate(
            (
                (q_in.at[:, own_heads], qbuf.at[s]),
                (cache_in, kc.at[k]),
                (uv_in.at[own_heads], wuv),
                (out_in, wout.at[own_units]),
                (router_in.at[:, pl.ds(first_column, COLS)], rpad.at[pl.ds(0, 16)]),
                (gate_in, wgate.at[k]),
                (up_in, wup.at[k]),
                (down_in, wdown.at[own_units]),
            )
        )
    ]
    for n in (0, 1, 2):
        loads[n].start()

    barrier = pltpu.get_barrier_semaphore()
    partners = [member((s + r) % 16) for r in range(1, 16)]
    planes = [(dx, dy, dz) for dx in range(4) for dy in range(4) for dz in range(4) if 0 in (dx, dy, dz)]
    for dx, dy, dz in planes:
        if dx:
            partners.append(device((x + dx) % 4, (y + dy) % 4, (z + dz) % 4, k))
        elif dz in (1, 3):
            if dz == 1:
                partners.append(device(x, (y + dy) % 4, (1 - zh) * 2, k))
            else:
                partners.append(device(x, (y + dy) % 4, (1 - zh) * 2 + 1, k))
    for there in partners:
        pl.semaphore_signal(barrier, inc=1, device_id=there, device_id_type=MESH)
    pl.semaphore_wait(barrier, len(partners))

    links = Links(send_sem, recv_sem, other)
    send, arrived, slots = links.send, links.arrived, links.slots

    q_slot = slots(16)
    k_slot = slots(2)
    for dy in (0, 3, 1, 2):
        for dz in (0, 1):
            for dk in (1, 0):
                if (dy, dz, dk) == (0, 0, 0):
                    continue
                kk = (k + dk) % 2
                t = ((y + dy) % 4) * 4 + ((zl + dz) % 2) * 2 + kk
                heads = pl.ds(pl.multiple_of(kk * 16, 16), 16)
                send(q_in.at[:, heads], qbuf.at[s], q_slot + s, member(t))
        if dy == 0:
            send(cache_in, kc.at[k], k_slot, other)

    fresh = new_keys[...].astype(F32)
    row = lax.broadcasted_iota(jnp.int32, (16, 576), 0)
    kn[own_heads] = jnp.where(
        row == 0, fresh[0:1, :], jnp.where(row == 1, fresh[1:2, :], 0.0)
    ).astype(BF16)
    send(kn.at[own_heads], kn.at[own_heads], k_slot + 1, other)
    kn[pl.ds(32, 96)] = jnp.zeros((96, 576), BF16)
    rpad[pl.ds(16, 112)] = jnp.zeros((112, COLS), BF16)

    extra_row = lax.broadcasted_iota(jnp.int32, (16, 7168), 0)
    rest = residual[...].astype(F32)
    extra[k, :, pl.ds(0, 7168)] = jnp.where(
        extra_row == 0, rest[0:1, :], jnp.where(extra_row == 1, rest[1:2, :], 0.0)
    ).astype(BF16)
    note_row = lax.broadcasted_iota(jnp.int32, (16, 128), 0)
    note_lane = lax.broadcasted_iota(jnp.int32, (16, 128), 1)
    own_ids = ids[...]
    facts = jnp.zeros((16, 128), F32)
    for t in range(2):
        mark = jnp.zeros((16, 128), F32)
        for j in range(8):
            mark = mark + jnp.where(note_lane == own_ids[t : t + 1, j : j + 1] + 48, 0.125, 0.0)
        keep = jnp.ones((1, 1), F32) if t == 0 else accept[...].astype(F32)
        mark = mark + jnp.where(note_lane == 65, keep, 0.0)
        facts = jnp.where(note_row == t, mark, facts)
    extra[k, :, pl.ds(7168, 128)] = facts.astype(BF16)
    e_slot = slots(1)
    send(extra.at[k], extra.at[k], e_slot, other)

    to_log2 = score_scale * log2e

    def attend(ya, yb, own):
        for yy in (ya, yb):
            for n in range(4):
                t = yy * 4 + n
                if own and yy is y:
                    t = y * 4 + (zl * 2 + k + n) % 4
                    if n == 0:
                        continue
                arrived(qbuf.at[t], q_slot + t)
        q = jnp.concatenate(
            [qbuf[pl.ds(yy * 4, 4)].reshape(128, 576) for yy in (ya, yb)], axis=0
        )
        scores = [mm(q, kc[n]) * to_log2 for n in range(2)]
        peaks = [jnp.max(part, axis=1, keepdims=True) for part in scores]
        peak = jnp.maximum(peaks[0], peaks[1])
        if own:
            row = lax.broadcasted_iota(jnp.int32, (256, 128), 0) - zl * 64
            column = lax.broadcasted_iota(jnp.int32, (256, 128), 1)
            seen = (
                (row >= 0)
                & (row < 64)
                & ((column >> 4) == (row >> 5))
                & ((column & 15) <= ((row >> 4) & 1))
            )
            own_scores = jnp.where(seen, nt(q, kn[...]) * to_log2, -jnp.inf)
            peak = jnp.maximum(peak, jnp.max(own_scores, axis=1, keepdims=True))
        denom = jnp.zeros((256, 1), F32)
        latent = jnp.zeros((256, 512), F32)
        for n in range(2):
            weights = jnp.exp2(scores[n] - peak)
            denom = denom + jnp.sum(weights, axis=1, keepdims=True)
            latent = latent + nt(weights.astype(BF16), kc[n, pl.ds(0, 512), :])
        if own:
            own_weights = jnp.exp2(own_scores - peak)
            denom = denom + jnp.sum(own_weights, axis=1, keepdims=True)
            latent = latent + mm(own_weights.astype(BF16), kn[:, pl.ds(0, 512)])
        latent = latent / denom
        level = jnp.broadcast_to(peak + jnp.log2(denom), (256, 128))
        for i, yy in enumerate((ya, yb)):
            at_rows = pl.ds(pl.multiple_of(yy * 128, 128), 128)
            for n in range(4):
                obuf[n, at_rows, :] = latent[i * 128 : i * 128 + 128, n * 128 : n * 128 + 128]
            obuf[4, at_rows, :] = level[i * 128 : i * 128 + 128]

    loads[0].wait()
    loads[1].wait()
    arrived(kn.at[pl.ds(pl.multiple_of(16 - k * 16, 16), 16)], k_slot + 1)
    arrived(kc.at[1 - k], k_slot)
    for n in (3, 4, 5, 6, 7):
        loads[n].start()
    w_slot = slots(4)
    send(out_in, wout.at[own_units], w_slot + 3, other)
    send(gate_in, wgate.at[k], w_slot, other)
    send(up_in, wup.at[k], w_slot + 1, other)
    send(down_in, wdown.at[own_units], w_slot + 2, other)
    attend(y, (y + 1) % 4, True)
    attend((y + 3) % 4, (y + 2) % 4, False)

    targets = assign[...]
    places = ((targets >> 1) & 1) * 16 + (targets >> 2) * 2 + (targets & 1)
    move = (lax.broadcasted_iota(jnp.int32, (32, 32), 0) == places).astype(BF16)
    spots = lax.broadcasted_iota(jnp.int32, (1, 32), 1)

    lane32 = lax.broadcasted_iota(jnp.int32, (32, 128), 1)
    v_slot = slots(8)
    own_share = (chip // 4) == k
    loads[2].wait()
    for r in (2, 1, 3, 0):
        local_chip = (chip + r) % 4
        there = k * 4 + local_chip
        stats = jnp.zeros((32, 128), F32)
        shares = []
        for j in range(4):
            head = local_chip * 4 + j
            mine = [obuf[n, pl.ds(head, 32, stride=16), :] for n in range(5)]
            latent = jnp.concatenate(mine[:4], axis=1).astype(BF16)
            shares.append(mm(latent, wuv[head]).astype(BF16))
            level = mine[4]
            high = level.astype(BF16).astype(F32)
            middle = (level - high).astype(BF16).astype(F32)
            low = level - high - middle
            stats = jnp.where(lane32 == j * 32, high, stats)
            stats = jnp.where(lane32 == j * 32 + 1, middle, stats)
            stats = jnp.where(lane32 == j * 32 + 2, low, stats)
        message = jnp.concatenate(shares + [stats.astype(BF16)], axis=1)
        vsend[r] = mm(move, message).astype(BF16).reshape(2, 16, 640)
        send(vsend.at[r, 1 - k], vrecv.at[chip], v_slot + chip, member(there * 2 + 1 - k))
        if r:
            send(vsend.at[r, k], vrecv.at[chip], v_slot + chip, member(there * 2 + k))
    own_send = pltpu.make_async_remote_copy(
        src_ref=vsend.at[0, k],
        dst_ref=vrecv.at[chip],
        send_sem=load_sem.at[8],
        recv_sem=recv_sem.at[v_slot + chip],
        device_id=member((k * 4 + chip % 4) * 2 + k),
        device_id_type=MESH,
    )

    @pl.when(own_share)
    def _():
        vrecv[chip] = vsend[0, k]

    @pl.when(jnp.logical_not(own_share))
    def _():
        own_send.start()

    for r in range(1, 8):
        c = (chip + r) % 8
        arrived(vrecv.at[c], v_slot + c)

    @pl.when(jnp.logical_not(own_share))
    def _():
        arrived(vrecv.at[chip], v_slot + chip)
        own_send.wait_send()

    lane3 = lax.broadcasted_iota(jnp.int32, (8, 16, 128), 2)
    got = vrecv[:, :, pl.ds(512, 128)].astype(F32)
    values = []
    for j in range(4):
        inside = (lane3 >= j * 32) & (lane3 < j * 32 + 3)
        level = jnp.sum(jnp.where(inside, got, 0.0), axis=2, keepdims=True)
        share = jnp.exp2(level - jnp.max(level, axis=0, keepdims=True))
        total = jnp.sum(share, axis=0)
        heard = vrecv[:, :, pl.ds(j * 128, 128)].astype(F32)
        values.append(jnp.sum(heard * share, axis=0) / total)
    values = jnp.concatenate(values, axis=1).astype(BF16)

    a_slot = slots(8)
    loads[3].wait()
    arrived(wout.at[pl.ds(pl.multiple_of(256 - k * 256, 256), 256)], w_slot + 3)
    arrived(extra.at[1 - k], e_slot)
    row_wide = lax.broadcasted_iota(jnp.int32, (16, COLS), 0)
    own_rows = []
    for kk in range(2):
        for t in range(2):
            spot = (chip * 2 + kk) * 2 + t
            place = jnp.sum(jnp.where(spots == spot, places, 0), axis=1, keepdims=True)
            own_rows.append((kk, t, place - k * 16))

    def with_extra(value, rows, columns):
        for kk in range(2):
            rest = extra[kk, :, columns].astype(F32)
            for other_kk, t, place in own_rows:
                if other_kk == kk:
                    value = value + jnp.where(rows == place, rest[t : t + 1, :], 0.0)
        return value

    facts = with_extra(jnp.zeros((16, 128), F32), note_row, pl.ds(7168, 128)).astype(BF16)
    for dy in (2, 1, 3, 0):
        for dz in (1, 0):
            c = ((y + dy) % 4) * 2 + (zl + dz) % 2
            columns = pl.ds(pl.multiple_of(c * COLS, 128), COLS)
            part = with_extra(mm(values, wout[:, columns]), row_wide, columns)
            part = jnp.concatenate([part.astype(BF16), facts], axis=1)
            if (dy, dz) == (0, 0):
                arecv[chip] = part
            else:
                n = dy * 2 + dz
                asend[n] = part
                send(asend.at[n], arecv.at[chip], a_slot + chip, member(c * 2 + k))
    for r in range(1, 8):
        c = (chip + r) % 8
        arrived(arecv.at[c], a_slot + c)
    total = jnp.sum(arecv[...].astype(F32), axis=0)
    hidden = total[:, :COLS].astype(BF16).astype(F32)
    facts = total[:, COLS:]
    keep = jnp.sum(jnp.where(note_lane == 65, facts, 0.0), axis=1, keepdims=True)

    loads[4].wait()
    gf[...] = gain[...].astype(F32)
    own_gain = jnp.concatenate([gf[pl.ds(chip * 7 + j, 1), :] for j in range(7)], axis=1)
    block = (hidden * own_gain).astype(BF16)
    squares = jnp.sum(hidden * hidden, axis=1, keepdims=True)
    squares_high = squares.astype(BF16).astype(F32)
    logits = nt(block, rpad[...])
    logits_high = logits.astype(BF16).astype(F32)
    note = logits_high + pltpu.roll(logits - logits_high, 16, 1) + facts
    note = note + jnp.where(note_lane == 32, squares_high, 0.0)
    note = note + jnp.where(note_lane == 33, squares - squares_high, 0.0)
    tail = jnp.concatenate([block[:, 768:], note.astype(BF16)], axis=1)
    gathered = (xa, xb, xc)
    for buf, (w, _, order), piece in zip(
        gathered, PIECES, (block[:, :384], block[:, 384:768], tail)
    ):
        c1, c2, c3 = (at[axis] for axis in order)
        buf[c3, c2, c1] = piece

    around = [(o1, o2) for o2 in (2, 1, 3, 0) for o1 in (2, 1, 3, 0) if (o1, o2) != (0, 0)]
    plan = []
    for buf, (w, _, order) in zip(gathered, PIECES):
        plan.append((buf, order, tuple(at[axis] for axis in order), slots(16), slots(6)))
    for o1, o2 in around:
        for buf, order, (c1, c2, c3), s1, s3 in plan:
            mine = buf.at[c3, c2, c1]
            send(mine, mine, s1 + o2 * 4 + o1, beside(order, o1, o2))

    kept = hidden * keep
    for j in range(7):
        f1[j] = kept[:, j * 128 : (j + 1) * 128]
    f2[...] = jnp.zeros_like(f2)
    for t in range(2):
        for j in range(7):
            f2[pl.ds(t * 7 + j, 8, stride=16), :] = f1[j, pl.ds(t, 8, stride=2), :]
    fsend[...] = f2[...].reshape(8, 16, 128).astype(BF16)
    f_slot = slots(8)
    for r in range(1, 8):
        c = (chip + r) % 8
        send(fsend.at[c], frecv.at[chip], f_slot + chip, member(c * 2 + k))
    frecv[chip] = fsend[chip]

    for buf, order, (c1, c2, c3), s1, s3 in plan:
        for o1, o2 in reversed(around):
            arrived(buf.at[c3, (c2 + 4 - o2) % 4, (c1 + 4 - o1) % 4], s1 + o2 * 4 + o1)

    def half(buf, c3, h):
        return buf.at[c3, pl.ds(2 * h, 2)]

    for h, o in ((0, 1), (1, 3), (0, 3), (1, 1)):
        for buf, order, (c1, c2, c3), s1, s3 in plan:
            mine = half(buf, c3, h)
            send(mine, mine, s3 + (0 if o == 1 else 2) + h, peer(order[2], o))

    def rows_of(n, yy, zz, columns):
        blocks = []
        for hh in range(2):
            for xx in range(4):
                c = {"x": xx, "y": yy, "z": hh * 2 + zz}
                c1, c2, c3 = (c[axis] for axis in PIECES[n][2])
                blocks.append(gathered[n][c3, c2, c1, :, columns])
        return jnp.concatenate(blocks, axis=0)

    parts = [[jnp.zeros((128, 256), F32) for _ in range(2)] for _ in range(2)]

    def multiply(n, yy, first, width):
        for zz in range(2):
            tokens = rows_of(n, yy, zz, pl.ds(0, width))
            at_rows = pl.ds(pl.multiple_of((yy * 2 + zz) * COLS + first, 128), width)
            for b in range(2):
                parts[b][0] = parts[b][0] + mm(tokens, wgate[b, at_rows, :])
                parts[b][1] = parts[b][1] + mm(tokens, wup[b, at_rows, :])

    loads[5].wait()
    loads[6].wait()
    arrived(wgate.at[1 - k], w_slot)
    arrived(wup.at[1 - k], w_slot + 1)
    multiply(0, y, 0, 384)
    for buf, order, (c1, c2, c3), s1, s3 in plan:
        for c, h, n, o in (((c3 + 3) % 4, 0, 0, 1), ((c3 + 1) % 4, 1, 3, 3)):
            view = half(buf, c, h)
            arrived(view, s3 + n)
            send(view, view, s3 + 4 + h, peer(order[2], o))

    def rest(n, last):
        buf, order, (c1, c2, c3), s1, s3 = plan[n]
        if last:
            arrived(half(buf, (c3 + 2) % 4, 0), s3 + 4)
            arrived(half(buf, (c3 + 2) % 4, 1), s3 + 5)
        else:
            arrived(half(buf, (c3 + 3) % 4, 1), s3 + 1)
            arrived(half(buf, (c3 + 1) % 4, 0), s3 + 2)

    rest(0, False)
    multiply(0, (y + 3) % 4, 0, 384)
    multiply(0, (y + 1) % 4, 0, 384)
    rest(0, True)
    multiply(0, (y + 2) % 4, 0, 384)
    rest(1, False)
    rest(1, True)
    for yy in range(4):
        multiply(1, yy, 384, 384)
    rest(2, False)
    rest(2, True)
    note = jnp.zeros((128, 128), F32)
    for yy in range(4):
        multiply(2, yy, 768, 128)
        for zz in range(2):
            note = note + rows_of(2, yy, zz, pl.ds(128, 128)).astype(F32)

    lane = lax.broadcasted_iota(jnp.int32, (128, 128), 1)

    def column_sum(inside):
        return jnp.sum(jnp.where(inside, note, 0.0), axis=1, keepdims=True)

    model_width = 8 * COLS
    scale = lax.rsqrt(column_sum((lane == 32) | (lane == 33)) / model_width + norm_eps)
    logits = (note + pltpu.roll(note, 112, 1)) * scale
    chosen = jnp.where(lane < 16, jax.nn.sigmoid(logits) * pltpu.roll(note, 80, 1), 0.0)
    expert = (p * 16 + s) // 8
    gate = jnp.sum(jnp.where(lane == expert, chosen, 0.0), axis=1, keepdims=True)
    gate = gate / jnp.sum(chosen, axis=1, keepdims=True) * route_scale
    gate = gate * column_sum(lane == 65) * 0.125
    act = [jax.nn.silu(g * scale) * (u * scale) * gate for g, u in parts]
    act = jnp.concatenate(act, axis=1).astype(BF16)
    to_row = lax.broadcasted_iota(jnp.int32, (128, 128), 0)
    from_row = ((to_row >> 3) & 7) * 16 + (to_row & 7) * 2 + (to_row >> 6)
    act = mm((from_row == lane).astype(BF16), act).astype(BF16)

    loads[7].wait()
    arrived(wdown.at[pl.ds(pl.multiple_of(256 - k * 256, 256), 256)], w_slot + 2)
    partial = (pa, pb, pc)

    def project(n):
        w, order = PIECES[n][1:]
        start = sum(other_piece[1] for other_piece in PIECES[:n])
        for c in range(8):
            part = mm(act, wdown[:, pl.ds(c * COLS + start, w)])
            for t in range(2):
                for j in range(w // 128):
                    block = part[t * 64 : t * 64 + 64, j * 128 : (j + 1) * 128]
                    stage[start // 128 + j, pl.ds(2 * c + t, 64, stride=16), :] = block
        for hh in range(2):
            for xx in range(4):
                for r in range(8):
                    at_block = {"x": xx, "y": r // 2, "z": hh * 2 + r % 2}
                    c1, c2, c3 = (at_block[axis] for axis in order)
                    rows = pl.ds(((hh * 4 + xx) * 8 + r) * 16, 16)
                    tiles = [stage[start // 128 + j, rows, :] for j in range(w // 128)]
                    partial[n][c3, c2, c1] = jnp.concatenate(tiles, axis=1).astype(BF16)

    plan = []
    for n, (_, w, order) in enumerate(PIECES):
        bufs = (partial[n], (r1a, r1b, r1c)[n], (r2a, r2b, r2c)[n])
        plan.append((bufs, order, tuple(at[axis] for axis in order), slots(6), slots(16)))

    def add_to(ref, *terms):
        total = ref[...].astype(F32)
        for term in terms:
            total = total + term[...].astype(F32)
        ref[...] = total.astype(BF16)

    def pass_on(piece, step):
        (part, r1, r2), order, (c1, c2, c3), s1, s2 = plan[piece]
        for n, (to, h, o) in enumerate(((2, 0, 1), (2, 1, 3), (1, 1, 1), (3, 0, 3))):
            if to == step:
                send(half(part, (c3 + step) % 4, h), r1.at[n], s1 + n, peer(order[2], o))

    for n in range(3):
        project(n)
        for step in (2, 1, 3):
            pass_on(n, step)
    for n, (step, h, o) in enumerate(((1, 0, 1), (3, 1, 3))):
        for (part, r1, r2), order, (c1, c2, c3), s1, s2 in plan:
            view = half(part, (c3 + step) % 4, h)
            arrived(r1.at[n], s1 + n)
            add_to(view, r1.at[n])
            send(view, r1.at[n + 4], s1 + n + 4, peer(order[2], o))
    for (part, r1, r2), order, (c1, c2, c3), s1, s2 in plan:
        for n in (2, 3, 4, 5):
            arrived(r1.at[n], s1 + n)
        add_to(half(part, c3, 0), r1.at[3], r1.at[4])
        add_to(half(part, c3, 1), r1.at[2], r1.at[5])
        for o1, o2 in around:
            block = part.at[c3, (c2 + o2) % 4, (c1 + o1) % 4]
            send(block, r2.at[o2 * 4 + o1], s2 + o2 * 4 + o1, beside(order, o1, o2))

    for r in range(1, 8):
        c = (chip + r) % 8
        arrived(frecv.at[c], f_slot + c)
    f2[...] = frecv[...].reshape(128, 128).astype(F32)

    sums = []
    for (part, r1, r2), order, (c1, c2, c3), s1, s2 in plan:
        for o1, o2 in reversed(around):
            arrived(r2.at[o2 * 4 + o1], s2 + o2 * 4 + o1)
        got = r2[pl.ds(1, 15)].astype(F32)
        sums.append(part[c3, c2, c1].astype(F32) + jnp.sum(got, axis=0))
    final = jnp.concatenate(sums, axis=1)
    for j in range(7):
        f1[j] = final[:, j * 128 : (j + 1) * 128]
    rows = [
        f1[j, pl.ds(2 * c, 2), :] + f2[pl.ds(c * 16 + j, 2, stride=7), :]
        for c in range(8)
        for j in range(7)
    ]
    result[...] = jnp.concatenate(rows, axis=1).astype(BF16)
    links.finish()


def local(
    queries,
    new_keys,
    cache,
    residual,
    w_uv,
    w_out,
    norm_gain,
    router,
    expert_ids,
    w_gate,
    w_up,
    w_down,
    accept,
    assign,
):
    positions = cache.shape[1]
    whole = pl.BlockSpec(memory_space=pltpu.VMEM)
    left = pl.BlockSpec(memory_space=pl.ANY)
    scratch = [
        pltpu.VMEM((2, 576, positions), BF16),
        pltpu.VMEM((16, 512, 128), BF16),
        pltpu.VMEM((512, 7168), BF16),
        pltpu.VMEM((2, 7168, 256), BF16),
        pltpu.VMEM((2, 7168, 256), BF16),
        pltpu.VMEM((512, 7168), BF16),
        pltpu.VMEM((128, COLS), BF16),
        pltpu.VMEM((16, 2, 16, 576), BF16),
        pltpu.VMEM((128, 576), BF16),
        pltpu.VMEM((5, 512, 128), F32),
        pltpu.VMEM((4, 2, 16, 640), BF16),
        pltpu.VMEM((8, 16, 640), BF16),
        pltpu.VMEM((8, 16, COLS + 128), BF16),
        pltpu.VMEM((8, 16, COLS + 128), BF16),
        pltpu.VMEM((7, 1024, 128), F32),
    ]
    scratch += [pltpu.VMEM((4, 4, 4, 16, w), BF16) for w, _, _ in PIECES]
    scratch += [pltpu.VMEM((4, 4, 4, 16, w), BF16) for _, w, _ in PIECES]
    scratch += [pltpu.VMEM((6, 2, 4, 16, w), BF16) for _, w, _ in PIECES]
    scratch += [pltpu.VMEM((16, 16, w), BF16) for _, w, _ in PIECES]
    scratch += [
        pltpu.VMEM((7, 16, 128), F32),
        pltpu.VMEM((128, 128), F32),
        pltpu.VMEM((8, 16, 128), BF16),
        pltpu.VMEM((8, 16, 128), BF16),
        pltpu.VMEM((56, 128), F32),
        pltpu.VMEM((2, 16, 7296), BF16),
        pltpu.SemaphoreType.DMA((9,)),
        pltpu.SemaphoreType.DMA((192,)),
        pltpu.SemaphoreType.DMA((192,)),
    ]
    rows = pl.pallas_call(
        kernel,
        out_shape=jax.ShapeDtypeStruct((2, 7168), BF16),
        in_specs=[left] * 8 + [whole] * 6,
        out_specs=whole,
        scratch_shapes=scratch,
        compiler_params=pltpu.CompilerParams(
            collective_id=0, has_side_effects=True, vmem_limit_bytes=60 * 1024 * 1024
        ),
        name="layer",
    )(
        queries,
        cache[0].T,
        w_uv,
        w_out,
        router.T,
        w_gate[0],
        w_up[0],
        w_down[0],
        new_keys,
        residual,
        norm_gain.reshape(56, 128),
        expert_ids,
        accept,
        assign,
    )
    return rows


def solution(mesh):
    placed = (
        P(("prompt", "sample"), None, None),
        P(("prompt", "sample"), None),
        P("prompt", "sample", None),
        P(("prompt", "sample"), None),
        P(),
        P("sample", None),
        P(),
        P(),
        P(("prompt", "sample"), None),
        P(("prompt", "sample"), None, None),
        P(("prompt", "sample"), None, None),
        P(("prompt", "sample"), None, None),
        P("prompt", "sample"),
        P("prompt", None),
    )
    return jax.shard_map(
        local, mesh=mesh, in_specs=placed, out_specs=P(("prompt", "sample"), None), check_vma=False
    )
```

```python
import functools
import jax
import jax.numpy as jnp
from jax import lax
from jax.experimental import pallas as pl
from jax.experimental.pallas import tpu as pltpu
from jax.sharding import PartitionSpec as P

MESH = pl.DeviceIdType.MESH
F32 = jnp.float32
BF16 = jnp.bfloat16
score_scale = 192.0 ** (-0.5)
log2e = 1.4426950408889634
route_scale = 2.827
norm_eps = 1e-06

COLS = 896
PIECES = ((384, 384, "xzy"), (384, 256, "yxz"), (256, 256, "zyx"))


def nt(a, b):
    return lax.dot_general(a, b, (((1,), (1,)), ((), ())), preferred_element_type=F32)


def mm(a, b):
    return jnp.dot(a, b, preferred_element_type=F32)


class Links:
    def __init__(self, send_sem, recv_sem, anyone):
        self.send_sem, self.recv_sem, self.anyone = send_sem, recv_sem, anyone
        self.sent, self.taken = [], 0

    def slots(self, n=1):
        self.taken += n
        return self.taken - n

    def send(self, src, dst, slot, device):
        copy = pltpu.make_async_remote_copy(
            src_ref=src,
            dst_ref=dst,
            send_sem=self.send_sem.at[len(self.sent)],
            recv_sem=self.recv_sem.at[slot],
            device_id=device,
            device_id_type=MESH,
        )
        copy.start()
        self.sent.append(copy)

    def arrived(self, dst, slot):
        pltpu.make_async_remote_copy(
            src_ref=dst,
            dst_ref=dst,
            send_sem=self.send_sem.at[0],
            recv_sem=self.recv_sem.at[slot],
            device_id=self.anyone,
            device_id_type=MESH,
        ).wait_recv()

    def finish(self):
        for copy in self.sent:
            copy.wait_send()


def kernel(
    q_in,
    cache_in,
    uv_in,
    out_in,
    router_in,
    gate_in,
    up_in,
    down_in,
    new_keys,
    residual,
    gain,
    ids,
    accept,
    assign,
    result,
    kc,
    wuv,
    wout,
    wgate,
    wup,
    wdown,
    rpad,
    qbuf,
    kn,
    obuf,
    vsend,
    vrecv,
    asend,
    arecv,
    stage,
    xa,
    xb,
    xc,
    pa,
    pb,
    pc,
    r1a,
    r1b,
    r1c,
    r2a,
    r2b,
    r2c,
    ba,
    bb,
    bc,
    f1,
    f2,
    fsend,
    frecv,
    gf,
    extra,
    load_sem,
    send_sem,
    recv_sem,
):
    p = lax.axis_index("prompt")
    s = lax.axis_index("sample")
    x, zh = p // 2, p % 2
    y, zl, k = s // 4, (s // 2) % 2, s % 2
    z = zh * 2 + zl
    chip = y * 2 + zl
    at = {"x": x, "y": y, "z": z}

    def device(x, y, z, k):
        return (x * 2 + z // 2, y * 4 + (z % 2) * 2 + k)

    def peer(axis, step):
        there = dict(at)
        there[axis] = (at[axis] + step) % 4
        return device(there["x"], there["y"], there["z"], k)

    def beside(order, o1, o2):
        there = dict(at)
        there[order[0]] = (at[order[0]] + o1) % 4
        there[order[1]] = (at[order[1]] + o2) % 4
        return device(there["x"], there["y"], there["z"], k)

    def member(t):
        return (p, t)

    other = (p, y * 4 + zl * 2 + (1 - k))
    across = (p, y * 4 + (1 - zl) * 2 + k)

    first_column = pl.multiple_of(chip * COLS, 128)
    own_heads = pl.ds(pl.multiple_of(k * 16, 16), 16)
    own_units = pl.ds(pl.multiple_of(k * 256, 256), 256)
    loads = [
        pltpu.make_async_copy(src, dst, load_sem.at[n])
        for n, (src, dst) in enumerate(
            (
                (q_in.at[:, own_heads], qbuf.at[s]),
                (cache_in, kc.at[k]),
                (uv_in.at[own_heads], wuv),
                (out_in, wout.at[own_units]),
                (router_in.at[:, pl.ds(first_column, COLS)], rpad.at[pl.ds(0, 16)]),
                (gate_in, wgate.at[k]),
                (up_in, wup.at[k]),
                (down_in, wdown.at[own_units]),
            )
        )
    ]
    for n in (0, 1, 2):
        loads[n].start()

    barrier = pltpu.get_barrier_semaphore()
    partners = [member((s + r) % 16) for r in range(1, 16)]
    planes = [(dx, dy, dz) for dx in range(4) for dy in range(4) for dz in range(4) if 0 in (dx, dy, dz)]
    for dx, dy, dz in planes:
        if dx:
            partners.append(device((x + dx) % 4, (y + dy) % 4, (z + dz) % 4, k))
        elif dz in (1, 3):
            if dz == 1:
                partners.append(device(x, (y + dy) % 4, (1 - zh) * 2, k))
            else:
                partners.append(device(x, (y + dy) % 4, (1 - zh) * 2 + 1, k))
    for there in partners:
        pl.semaphore_signal(barrier, inc=1, device_id=there, device_id_type=MESH)
    pl.semaphore_wait(barrier, len(partners))

    links = Links(send_sem, recv_sem, other)
    send, arrived, slots = links.send, links.arrived, links.slots

    q_slot = slots(16)
    k_slot = slots(2)
    for dy in (0, 3, 1, 2):
        for dz in (0, 1):
            for dk in (1, 0):
                if (dy, dz, dk) == (0, 0, 0):
                    continue
                kk = (k + dk) % 2
                t = ((y + dy) % 4) * 4 + ((zl + dz) % 2) * 2 + kk
                heads = pl.ds(pl.multiple_of(kk * 16, 16), 16)
                send(q_in.at[:, heads], qbuf.at[s], q_slot + s, member(t))
        if dy == 0:
            send(cache_in, kc.at[k], k_slot, other)

    fresh = new_keys[...].astype(F32)
    row = lax.broadcasted_iota(jnp.int32, (16, 576), 0)
    kn[own_heads] = jnp.where(
        row == 0, fresh[0:1, :], jnp.where(row == 1, fresh[1:2, :], 0.0)
    ).astype(BF16)
    send(kn.at[own_heads], kn.at[own_heads], k_slot + 1, other)
    kn[pl.ds(32, 96)] = jnp.zeros((96, 576), BF16)
    rpad[pl.ds(16, 112)] = jnp.zeros((112, COLS), BF16)

    extra_row = lax.broadcasted_iota(jnp.int32, (16, 7168), 0)
    rest = residual[...].astype(F32)
    extra[k, :, pl.ds(0, 7168)] = jnp.where(
        extra_row == 0, rest[0:1, :], jnp.where(extra_row == 1, rest[1:2, :], 0.0)
    ).astype(BF16)
    note_row = lax.broadcasted_iota(jnp.int32, (16, 128), 0)
    note_lane = lax.broadcasted_iota(jnp.int32, (16, 128), 1)
    own_ids = ids[...]
    facts = jnp.zeros((16, 128), F32)
    for t in range(2):
        mark = jnp.zeros((16, 128), F32)
        for j in range(8):
            mark = mark + jnp.where(note_lane == own_ids[t : t + 1, j : j + 1] + 48, 0.125, 0.0)
        keep = jnp.ones((1, 1), F32) if t == 0 else accept[...].astype(F32)
        mark = mark + jnp.where(note_lane == 65, keep, 0.0)
        facts = jnp.where(note_row == t, mark, facts)
    extra[k, :, pl.ds(7168, 128)] = facts.astype(BF16)
    e_slot = slots(1)
    send(extra.at[k], extra.at[k], e_slot, other)

    to_log2 = score_scale * log2e

    def attend(ya, yb, own):
        for yy in (ya, yb):
            for n in range(4):
                t = yy * 4 + n
                if own and yy is y:
                    t = y * 4 + (zl * 2 + k + n) % 4
                    if n == 0:
                        continue
                arrived(qbuf.at[t], q_slot + t)
        q = jnp.concatenate(
            [qbuf[pl.ds(yy * 4, 4)].reshape(128, 576) for yy in (ya, yb)], axis=0
        )
        scores = [mm(q, kc[n]) * to_log2 for n in range(2)]
        peaks = [jnp.max(part, axis=1, keepdims=True) for part in scores]
        peak = jnp.maximum(peaks[0], peaks[1])
        if own:
            row = lax.broadcasted_iota(jnp.int32, (256, 128), 0) - zl * 64
            column = lax.broadcasted_iota(jnp.int32, (256, 128), 1)
            seen = (
                (row >= 0)
                & (row < 64)
                & ((column >> 4) == (row >> 5))
                & ((column & 15) <= ((row >> 4) & 1))
            )
            own_scores = jnp.where(seen, nt(q, kn[...]) * to_log2, -jnp.inf)
            peak = jnp.maximum(peak, jnp.max(own_scores, axis=1, keepdims=True))
        denom = jnp.zeros((256, 1), F32)
        latent = jnp.zeros((256, 512), F32)
        for n in range(2):
            weights = jnp.exp2(scores[n] - peak)
            denom = denom + jnp.sum(weights, axis=1, keepdims=True)
            latent = latent + nt(weights.astype(BF16), kc[n, pl.ds(0, 512), :])
        if own:
            own_weights = jnp.exp2(own_scores - peak)
            denom = denom + jnp.sum(own_weights, axis=1, keepdims=True)
            latent = latent + mm(own_weights.astype(BF16), kn[:, pl.ds(0, 512)])
        latent = latent / denom
        level = jnp.broadcast_to(peak + jnp.log2(denom), (256, 128))
        for i, yy in enumerate((ya, yb)):
            at_rows = pl.ds(pl.multiple_of(yy * 128, 128), 128)
            for n in range(4):
                obuf[n, at_rows, :] = latent[i * 128 : i * 128 + 128, n * 128 : n * 128 + 128]
            obuf[4, at_rows, :] = level[i * 128 : i * 128 + 128]

    loads[0].wait()
    loads[1].wait()
    arrived(kn.at[pl.ds(pl.multiple_of(16 - k * 16, 16), 16)], k_slot + 1)
    arrived(kc.at[1 - k], k_slot)
    for n in (3, 4, 5, 6, 7):
        loads[n].start()
    w_slot = slots(4)
    send(out_in, wout.at[own_units], w_slot + 3, other)
    send(gate_in, wgate.at[k], w_slot, other)
    send(up_in, wup.at[k], w_slot + 1, other)
    send(down_in, wdown.at[own_units], w_slot + 2, other)
    attend(y, (y + 1) % 4, True)
    attend((y + 3) % 4, (y + 2) % 4, False)

    targets = assign[...]
    places = ((targets >> 1) & 1) * 16 + (targets >> 2) * 2 + (targets & 1)
    move = (lax.broadcasted_iota(jnp.int32, (32, 32), 0) == places).astype(BF16)
    spots = lax.broadcasted_iota(jnp.int32, (1, 32), 1)

    lane32 = lax.broadcasted_iota(jnp.int32, (32, 128), 1)
    v_slot = slots(8)
    own_share = (chip // 4) == k
    loads[2].wait()
    for r in (2, 1, 3, 0):
        local_chip = (chip + r) % 4
        there = k * 4 + local_chip
        stats = jnp.zeros((32, 128), F32)
        shares = []
        for j in range(4):
            head = local_chip * 4 + j
            mine = [obuf[n, pl.ds(head, 32, stride=16), :] for n in range(5)]
            latent = jnp.concatenate(mine[:4], axis=1).astype(BF16)
            shares.append(mm(latent, wuv[head]).astype(BF16))
            level = mine[4]
            high = level.astype(BF16).astype(F32)
            middle = (level - high).astype(BF16).astype(F32)
            low = level - high - middle
            stats = jnp.where(lane32 == j * 32, high, stats)
            stats = jnp.where(lane32 == j * 32 + 1, middle, stats)
            stats = jnp.where(lane32 == j * 32 + 2, low, stats)
        message = jnp.concatenate(shares + [stats.astype(BF16)], axis=1)
        vsend[r] = mm(move, message).astype(BF16).reshape(2, 16, 640)
        send(vsend.at[r, 1 - k], vrecv.at[chip], v_slot + chip, member(there * 2 + 1 - k))
        if r:
            send(vsend.at[r, k], vrecv.at[chip], v_slot + chip, member(there * 2 + k))
    own_send = pltpu.make_async_remote_copy(
        src_ref=vsend.at[0, k],
        dst_ref=vrecv.at[chip],
        send_sem=load_sem.at[8],
        recv_sem=recv_sem.at[v_slot + chip],
        device_id=member((k * 4 + chip % 4) * 2 + k),
        device_id_type=MESH,
    )

    @pl.when(own_share)
    def _():
        vrecv[chip] = vsend[0, k]

    @pl.when(jnp.logical_not(own_share))
    def _():
        own_send.start()

    for r in range(1, 8):
        c = (chip + r) % 8
        arrived(vrecv.at[c], v_slot + c)

    @pl.when(jnp.logical_not(own_share))
    def _():
        arrived(vrecv.at[chip], v_slot + chip)
        own_send.wait_send()

    lane3 = lax.broadcasted_iota(jnp.int32, (8, 16, 128), 2)
    got = vrecv[:, :, pl.ds(512, 128)].astype(F32)
    values = []
    for j in range(4):
        inside = (lane3 >= j * 32) & (lane3 < j * 32 + 3)
        level = jnp.sum(jnp.where(inside, got, 0.0), axis=2, keepdims=True)
        share = jnp.exp2(level - jnp.max(level, axis=0, keepdims=True))
        total = jnp.sum(share, axis=0)
        heard = vrecv[:, :, pl.ds(j * 128, 128)].astype(F32)
        values.append(jnp.sum(heard * share, axis=0) / total)
    values = jnp.concatenate(values, axis=1).astype(BF16)

    a_slot = slots(8)
    loads[3].wait()
    arrived(wout.at[pl.ds(pl.multiple_of(256 - k * 256, 256), 256)], w_slot + 3)
    arrived(extra.at[1 - k], e_slot)
    row_wide = lax.broadcasted_iota(jnp.int32, (16, COLS), 0)
    own_rows = []
    for kk in range(2):
        for t in range(2):
            spot = (chip * 2 + kk) * 2 + t
            place = jnp.sum(jnp.where(spots == spot, places, 0), axis=1, keepdims=True)
            own_rows.append((kk, t, place - k * 16))

    def with_extra(value, rows, columns):
        for kk in range(2):
            rest = extra[kk, :, columns].astype(F32)
            for other_kk, t, place in own_rows:
                if other_kk == kk:
                    value = value + jnp.where(rows == place, rest[t : t + 1, :], 0.0)
        return value

    facts = with_extra(jnp.zeros((16, 128), F32), note_row, pl.ds(7168, 128)).astype(BF16)
    for dy in (2, 1, 3, 0):
        for dz in (1, 0):
            c = ((y + dy) % 4) * 2 + (zl + dz) % 2
            columns = pl.ds(pl.multiple_of(c * COLS, 128), COLS)
            part = with_extra(mm(values, wout[:, columns]), row_wide, columns)
            part = jnp.concatenate([part.astype(BF16), facts], axis=1)
            if (dy, dz) == (0, 0):
                arecv[chip] = part
            else:
                n = dy * 2 + dz
                asend[n] = part
                send(asend.at[n], arecv.at[chip], a_slot + chip, member(c * 2 + k))
    for r in range(1, 8):
        c = (chip + r) % 8
        arrived(arecv.at[c], a_slot + c)
    total = jnp.sum(arecv[...].astype(F32), axis=0)
    hidden = total[:, :COLS].astype(BF16).astype(F32)
    facts = total[:, COLS:]
    keep = jnp.sum(jnp.where(note_lane == 65, facts, 0.0), axis=1, keepdims=True)

    loads[4].wait()
    gf[...] = gain[...].astype(F32)
    own_gain = jnp.concatenate([gf[pl.ds(chip * 7 + j, 1), :] for j in range(7)], axis=1)
    block = (hidden * own_gain).astype(BF16)
    squares = jnp.sum(hidden * hidden, axis=1, keepdims=True)
    squares_high = squares.astype(BF16).astype(F32)
    logits = nt(block, rpad[...])
    logits_high = logits.astype(BF16).astype(F32)
    note = logits_high + pltpu.roll(logits - logits_high, 16, 1) + facts
    note = note + jnp.where(note_lane == 32, squares_high, 0.0)
    note = note + jnp.where(note_lane == 33, squares - squares_high, 0.0)
    tail = jnp.concatenate([block[:, 768:], note.astype(BF16)], axis=1)
    gathered = (xa, xb, xc)
    for buf, (w, _, order), piece in zip(
        gathered, PIECES, (block[:, :384], block[:, 384:768], tail)
    ):
        c1, c2, c3 = (at[axis] for axis in order)
        buf[c3, c2, c1] = piece

    around = [(o1, o2) for o2 in (2, 1, 3, 0) for o1 in (2, 1, 3, 0) if (o1, o2) != (0, 0)]
    plan = []
    for buf, (w, _, order) in zip(gathered, PIECES):
        plan.append((buf, order, tuple(at[axis] for axis in order), slots(16), slots(6)))
    for o1, o2 in around:
        for buf, order, (c1, c2, c3), s1, s3 in plan:
            mine = buf.at[c3, c2, c1]
            send(mine, mine, s1 + o2 * 4 + o1, beside(order, o1, o2))

    kept = hidden * keep
    for j in range(7):
        f1[j] = kept[:, j * 128 : (j + 1) * 128]
    f2[...] = jnp.zeros_like(f2)
    for t in range(2):
        for j in range(7):
            f2[pl.ds(t * 7 + j, 8, stride=16), :] = f1[j, pl.ds(t, 8, stride=2), :]
    fsend[...] = f2[...].reshape(8, 16, 128).astype(BF16)
    f_slot = slots(8)
    for r in range(1, 8):
        c = (chip + r) % 8
        send(fsend.at[c], frecv.at[chip], f_slot + chip, member(c * 2 + k))
    frecv[chip] = fsend[chip]

    for buf, order, (c1, c2, c3), s1, s3 in plan:
        for o1, o2 in reversed(around):
            arrived(buf.at[c3, (c2 + 4 - o2) % 4, (c1 + 4 - o1) % 4], s1 + o2 * 4 + o1)

    def half(buf, c3, h, size=2):
        return buf.at[c3, pl.ds(size * h, size)]

    for h, o in ((0, 1), (1, 3), (0, 3), (1, 1)):
        for buf, order, (c1, c2, c3), s1, s3 in plan:
            mine = half(buf, c3, h)
            send(mine, mine, s3 + (0 if o == 1 else 2) + h, peer(order[2], o))

    def rows_of(n, yy, zz, columns):
        blocks = []
        for hh in range(2):
            for xx in range(4):
                c = {"x": xx, "y": yy, "z": hh * 2 + zz}
                c1, c2, c3 = (c[axis] for axis in PIECES[n][2])
                blocks.append(gathered[n][c3, c2, c1, :, columns])
        return jnp.concatenate(blocks, axis=0)

    parts = [[jnp.zeros((128, 256), F32) for _ in range(2)] for _ in range(2)]

    def multiply(n, yy, first, width):
        for zz in range(2):
            tokens = rows_of(n, yy, zz, pl.ds(0, width))
            at_rows = pl.ds(pl.multiple_of((yy * 2 + zz) * COLS + first, 128), width)
            for b in range(2):
                parts[b][0] = parts[b][0] + mm(tokens, wgate[b, at_rows, :])
                parts[b][1] = parts[b][1] + mm(tokens, wup[b, at_rows, :])

    loads[5].wait()
    loads[6].wait()
    arrived(wgate.at[1 - k], w_slot)
    arrived(wup.at[1 - k], w_slot + 1)
    multiply(0, y, 0, 384)
    for buf, order, (c1, c2, c3), s1, s3 in plan:
        for c, h, n, o in (((c3 + 3) % 4, 0, 0, 1), ((c3 + 1) % 4, 1, 3, 3)):
            view = half(buf, c, h)
            arrived(view, s3 + n)
            send(view, view, s3 + 4 + h, peer(order[2], o))

    def rest(n, last):
        buf, order, (c1, c2, c3), s1, s3 = plan[n]
        if last:
            arrived(half(buf, (c3 + 2) % 4, 0), s3 + 4)
            arrived(half(buf, (c3 + 2) % 4, 1), s3 + 5)
        else:
            arrived(half(buf, (c3 + 3) % 4, 1), s3 + 1)
            arrived(half(buf, (c3 + 1) % 4, 0), s3 + 2)

    rest(0, False)
    multiply(0, (y + 3) % 4, 0, 384)
    multiply(0, (y + 1) % 4, 0, 384)
    rest(0, True)
    multiply(0, (y + 2) % 4, 0, 384)
    rest(1, False)
    rest(1, True)
    for yy in range(4):
        multiply(1, yy, 384, 384)
    rest(2, False)
    rest(2, True)
    note = jnp.zeros((128, 128), F32)
    for yy in range(4):
        multiply(2, yy, 768, 128)
        for zz in range(2):
            note = note + rows_of(2, yy, zz, pl.ds(128, 128)).astype(F32)

    lane = lax.broadcasted_iota(jnp.int32, (128, 128), 1)

    def column_sum(inside):
        return jnp.sum(jnp.where(inside, note, 0.0), axis=1, keepdims=True)

    model_width = 8 * COLS
    scale = lax.rsqrt(column_sum((lane == 32) | (lane == 33)) / model_width + norm_eps)
    logits = (note + pltpu.roll(note, 112, 1)) * scale
    chosen = jnp.where(lane < 16, jax.nn.sigmoid(logits) * pltpu.roll(note, 80, 1), 0.0)
    expert = (p * 16 + s) // 8
    gate = jnp.sum(jnp.where(lane == expert, chosen, 0.0), axis=1, keepdims=True)
    gate = gate / jnp.sum(chosen, axis=1, keepdims=True) * route_scale
    gate = gate * column_sum(lane == 65) * 0.125
    act = [jax.nn.silu(g * scale) * (u * scale) * gate for g, u in parts]
    act = jnp.concatenate(act, axis=1).astype(BF16)
    loads[7].wait()
    arrived(wdown.at[pl.ds(pl.multiple_of(256 - k * 256, 256), 256)], w_slot + 2)
    partial = (pa, pb, pc)
    to_row = lax.broadcasted_iota(jnp.int32, (128, 128), 0)

    def project(n):
        w, order = PIECES[n][1:]
        owner = {axis: (to_row >> shift) & 3 for axis, shift in zip(order, (0, 2, 5))}
        prompt_row = ((owner["z"] >> 1) * 4 + owner["x"]) * 16
        from_row = prompt_row + (owner["y"] * 2 + (owner["z"] & 1)) * 2 + ((to_row >> 4) & 1)
        rows = mm((from_row == lane).astype(BF16), act).astype(BF16)
        start = sum(other_piece[1] for other_piece in PIECES[:n])
        for c in range(8):
            part = mm(rows, wdown[:, pl.ds(c * COLS + start, w)]).astype(BF16)
            for chunk in range(4):
                partial[n][chunk, c] = part[chunk * 32 : chunk * 32 + 32]

    plan = []
    for n, (_, w, order) in enumerate(PIECES):
        bufs = (partial[n], (r1a, r1b, r1c)[n], (r2a, r2b, r2c)[n])
        plan.append((bufs, order, tuple(at[axis] for axis in order), slots(6), slots(16)))

    def add_to(ref, *terms):
        total = ref[...].astype(F32)
        for term in terms:
            total = total + term[...].astype(F32)
        ref[...] = total.astype(BF16)

    blocks = (ba, bb, bc)

    def pass_on(piece, step):
        (part, r1, r2), order, (c1, c2, c3), s1, s2 = plan[piece]
        for n, (to, h, o) in enumerate(((2, 0, 1), (2, 1, 3), (1, 1, 1), (3, 0, 3))):
            if to == step:
                send(half(part, (c3 + step) % 4, h, 4), r1.at[n], s1 + n, peer(order[2], o))

    for n in range(3):
        project(n)
        for step in (2, 1, 3):
            pass_on(n, step)
    for n, (step, h, o) in enumerate(((1, 0, 1), (3, 1, 3))):
        for (part, r1, r2), order, (c1, c2, c3), s1, s2 in plan:
            view = half(part, (c3 + step) % 4, h, 4)
            arrived(r1.at[n], s1 + n)
            add_to(view, r1.at[n])
            send(view, r1.at[n + 4], s1 + n + 4, peer(order[2], o))
    for piece, ((part, r1, r2), order, (c1, c2, c3), s1, s2) in enumerate(plan):
        for n in (2, 3, 4, 5):
            arrived(r1.at[n], s1 + n)
        tiles = PIECES[piece][1] // 128
        for h, (one, two) in enumerate(((3, 4), (2, 5))):
            for i in range(4):
                c = h * 4 + i
                chunk = part[c3, c].astype(F32) + r1[one, i].astype(F32) + r1[two, i].astype(F32)
                for t in range(2):
                    for j in range(tiles):
                        stage[j, pl.ds(2 * c + t, 16, stride=16), :] = chunk[
                            t * 16 : t * 16 + 16, j * 128 : (j + 1) * 128
                        ]
        whole = jnp.concatenate([stage[j] for j in range(tiles)], axis=1)
        blocks[piece][...] = whole.astype(BF16).reshape(4, 4, 16, tiles * 128)
        for o1, o2 in around:
            block = blocks[piece].at[(c2 + o2) % 4, (c1 + o1) % 4]
            send(block, r2.at[o2 * 4 + o1], s2 + o2 * 4 + o1, beside(order, o1, o2))

    for r in range(1, 8):
        c = (chip + r) % 8
        arrived(frecv.at[c], f_slot + c)
    f2[...] = frecv[...].reshape(128, 128).astype(F32)

    sums = []
    for block, ((part, r1, r2), order, (c1, c2, c3), s1, s2) in zip(blocks, plan):
        for o1, o2 in reversed(around):
            arrived(r2.at[o2 * 4 + o1], s2 + o2 * 4 + o1)
        got = r2[pl.ds(1, 15)].astype(F32)
        sums.append(block[c2, c1].astype(F32) + jnp.sum(got, axis=0))
    final = jnp.concatenate(sums, axis=1)
    for j in range(7):
        f1[j] = final[:, j * 128 : (j + 1) * 128]
    rows = [
        f1[j, pl.ds(2 * c, 2), :] + f2[pl.ds(c * 16 + j, 2, stride=7), :]
        for c in range(8)
        for j in range(7)
    ]
    result[...] = jnp.concatenate(rows, axis=1).astype(BF16)
    links.finish()


def local(
    queries,
    new_keys,
    cache,
    residual,
    w_uv,
    w_out,
    norm_gain,
    router,
    expert_ids,
    w_gate,
    w_up,
    w_down,
    accept,
    assign,
):
    positions = cache.shape[1]
    whole = pl.BlockSpec(memory_space=pltpu.VMEM)
    left = pl.BlockSpec(memory_space=pl.ANY)
    scratch = [
        pltpu.VMEM((2, 576, positions), BF16),
        pltpu.VMEM((16, 512, 128), BF16),
        pltpu.VMEM((512, 7168), BF16),
        pltpu.VMEM((2, 7168, 256), BF16),
        pltpu.VMEM((2, 7168, 256), BF16),
        pltpu.VMEM((512, 7168), BF16),
        pltpu.VMEM((128, COLS), BF16),
        pltpu.VMEM((16, 2, 16, 576), BF16),
        pltpu.VMEM((128, 576), BF16),
        pltpu.VMEM((5, 512, 128), F32),
        pltpu.VMEM((4, 2, 16, 640), BF16),
        pltpu.VMEM((8, 16, 640), BF16),
        pltpu.VMEM((8, 16, COLS + 128), BF16),
        pltpu.VMEM((8, 16, COLS + 128), BF16),
        pltpu.VMEM((3, 256, 128), F32),
    ]
    scratch += [pltpu.VMEM((4, 4, 4, 16, w), BF16) for w, _, _ in PIECES]
    scratch += [pltpu.VMEM((4, 8, 32, w), BF16) for _, w, _ in PIECES]
    scratch += [pltpu.VMEM((6, 4, 32, w), BF16) for _, w, _ in PIECES]
    scratch += [pltpu.VMEM((16, 16, w), BF16) for _, w, _ in PIECES]
    scratch += [pltpu.VMEM((4, 4, 16, w), BF16) for _, w, _ in PIECES]
    scratch += [
        pltpu.VMEM((7, 16, 128), F32),
        pltpu.VMEM((128, 128), F32),
        pltpu.VMEM((8, 16, 128), BF16),
        pltpu.VMEM((8, 16, 128), BF16),
        pltpu.VMEM((56, 128), F32),
        pltpu.VMEM((2, 16, 7296), BF16),
        pltpu.SemaphoreType.DMA((9,)),
        pltpu.SemaphoreType.DMA((192,)),
        pltpu.SemaphoreType.DMA((192,)),
    ]
    rows = pl.pallas_call(
        kernel,
        out_shape=jax.ShapeDtypeStruct((2, 7168), BF16),
        in_specs=[left] * 8 + [whole] * 6,
        out_specs=whole,
        scratch_shapes=scratch,
        compiler_params=pltpu.CompilerParams(
            collective_id=0, has_side_effects=True, vmem_limit_bytes=60 * 1024 * 1024
        ),
        name="layer",
    )(
        queries,
        cache[0].T,
        w_uv,
        w_out,
        router.T,
        w_gate[0],
        w_up[0],
        w_down[0],
        new_keys,
        residual,
        norm_gain.reshape(56, 128),
        expert_ids,
        accept,
        assign,
    )
    return rows


def solution(mesh):
    placed = (
        P(("prompt", "sample"), None, None),
        P(("prompt", "sample"), None),
        P("prompt", "sample", None),
        P(("prompt", "sample"), None),
        P(),
        P("sample", None),
        P(),
        P(),
        P(("prompt", "sample"), None),
        P(("prompt", "sample"), None, None),
        P(("prompt", "sample"), None, None),
        P(("prompt", "sample"), None, None),
        P("prompt", "sample"),
        P("prompt", None),
    )
    return jax.shard_map(
        local, mesh=mesh, in_specs=placed, out_specs=P(("prompt", "sample"), None), check_vma=False
    )
```

```python
import functools
import jax
import jax.numpy as jnp
from jax import lax
from jax.experimental import pallas as pl
from jax.experimental.pallas import tpu as pltpu
from jax.sharding import PartitionSpec as P

MESH = pl.DeviceIdType.MESH
F32 = jnp.float32
BF16 = jnp.bfloat16
score_scale = 192.0 ** (-0.5)
log2e = 1.4426950408889634
route_scale = 2.827
norm_eps = 1e-06

COLS = 896
PIECES = ((384, 384, "xzy"), (384, 256, "yxz"), (256, 256, "zyx"))


def nt(a, b):
    return lax.dot_general(a, b, (((1,), (1,)), ((), ())), preferred_element_type=F32)


def mm(a, b):
    return jnp.dot(a, b, preferred_element_type=F32)


class Links:
    def __init__(self, send_sem, recv_sem, anyone):
        self.send_sem, self.recv_sem, self.anyone = send_sem, recv_sem, anyone
        self.sent, self.taken = [], 0

    def slots(self, n=1):
        self.taken += n
        return self.taken - n

    def send(self, src, dst, slot, device):
        copy = pltpu.make_async_remote_copy(
            src_ref=src,
            dst_ref=dst,
            send_sem=self.send_sem.at[len(self.sent)],
            recv_sem=self.recv_sem.at[slot],
            device_id=device,
            device_id_type=MESH,
        )
        copy.start()
        self.sent.append(copy)

    def arrived(self, dst, slot):
        pltpu.make_async_remote_copy(
            src_ref=dst,
            dst_ref=dst,
            send_sem=self.send_sem.at[0],
            recv_sem=self.recv_sem.at[slot],
            device_id=self.anyone,
            device_id_type=MESH,
        ).wait_recv()

    def finish(self):
        for copy in self.sent:
            copy.wait_send()


def kernel(
    q_in,
    cache_in,
    uv_in,
    out_in,
    router_in,
    gate_in,
    up_in,
    down_in,
    new_keys,
    residual,
    gain,
    ids,
    accept,
    assign,
    result,
    kc,
    wuv,
    wout,
    wgate,
    wup,
    wdown,
    rpad,
    qbuf,
    kn,
    obuf,
    vsend,
    vrecv,
    asend,
    arecv,
    stage,
    xa,
    xb,
    xc,
    pa,
    pb,
    pc,
    r1a,
    r1b,
    r1c,
    r2a,
    r2b,
    r2c,
    ba,
    bb,
    bc,
    f1,
    f2,
    fsend,
    frecv,
    gf,
    extra,
    load_sem,
    send_sem,
    recv_sem,
):
    p = lax.axis_index("prompt")
    s = lax.axis_index("sample")
    x, zh = p // 2, p % 2
    y, zl, k = s // 4, (s // 2) % 2, s % 2
    z = zh * 2 + zl
    chip = y * 2 + zl
    at = {"x": x, "y": y, "z": z}

    def device(x, y, z, k):
        return (x * 2 + z // 2, y * 4 + (z % 2) * 2 + k)

    def peer(axis, step):
        there = dict(at)
        there[axis] = (at[axis] + step) % 4
        return device(there["x"], there["y"], there["z"], k)

    def beside(order, o1, o2):
        there = dict(at)
        there[order[0]] = (at[order[0]] + o1) % 4
        there[order[1]] = (at[order[1]] + o2) % 4
        return device(there["x"], there["y"], there["z"], k)

    def member(t):
        return (p, t)

    other = (p, y * 4 + zl * 2 + (1 - k))
    across = (p, y * 4 + (1 - zl) * 2 + k)

    barrier = pltpu.get_barrier_semaphore()
    partners = [member((s + r) % 16) for r in range(1, 16)]
    planes = [(dx, dy, dz) for dx in range(4) for dy in range(4) for dz in range(4) if 0 in (dx, dy, dz)]
    for dx, dy, dz in planes:
        if dx:
            partners.append(device((x + dx) % 4, (y + dy) % 4, (z + dz) % 4, k))
        elif dz in (1, 3):
            if dz == 1:
                partners.append(device(x, (y + dy) % 4, (1 - zh) * 2, k))
            else:
                partners.append(device(x, (y + dy) % 4, (1 - zh) * 2 + 1, k))
    for there in partners:
        pl.semaphore_signal(barrier, inc=1, device_id=there, device_id_type=MESH)

    first_column = pl.multiple_of(chip * COLS, 128)
    own_heads = pl.ds(pl.multiple_of(k * 16, 16), 16)
    own_units = pl.ds(pl.multiple_of(k * 256, 256), 256)
    loads = [
        pltpu.make_async_copy(src, dst, load_sem.at[n])
        for n, (src, dst) in enumerate(
            (
                (q_in.at[:, own_heads], qbuf.at[s]),
                (cache_in, kc.at[k]),
                (uv_in.at[own_heads], wuv),
                (out_in, wout.at[own_units]),
                (router_in.at[:, pl.ds(first_column, COLS)], rpad.at[pl.ds(0, 16)]),
                (gate_in, wgate.at[k]),
                (up_in, wup.at[k]),
                (down_in, wdown.at[own_units]),
            )
        )
    ]
    for n in (0, 1, 2):
        loads[n].start()

    pl.semaphore_wait(barrier, len(partners))

    links = Links(send_sem, recv_sem, other)
    send, arrived, slots = links.send, links.arrived, links.slots

    q_slot = slots(16)
    k_slot = slots(2)
    for dy in (0, 3, 1, 2):
        for dz in (0, 1):
            for dk in (1, 0):
                if (dy, dz, dk) == (0, 0, 0):
                    continue
                kk = (k + dk) % 2
                t = ((y + dy) % 4) * 4 + ((zl + dz) % 2) * 2 + kk
                heads = pl.ds(pl.multiple_of(kk * 16, 16), 16)
                send(q_in.at[:, heads], qbuf.at[s], q_slot + s, member(t))
        if dy == 0:
            send(cache_in, kc.at[k], k_slot, other)

    fresh = new_keys[...].astype(F32)
    row = lax.broadcasted_iota(jnp.int32, (16, 576), 0)
    kn[own_heads] = jnp.where(
        row == 0, fresh[0:1, :], jnp.where(row == 1, fresh[1:2, :], 0.0)
    ).astype(BF16)
    send(kn.at[own_heads], kn.at[own_heads], k_slot + 1, other)
    kn[pl.ds(32, 96)] = jnp.zeros((96, 576), BF16)
    rpad[pl.ds(16, 112)] = jnp.zeros((112, COLS), BF16)

    extra_row = lax.broadcasted_iota(jnp.int32, (16, 7168), 0)
    rest = residual[...].astype(F32)
    extra[k, :, pl.ds(0, 7168)] = jnp.where(
        extra_row == 0, rest[0:1, :], jnp.where(extra_row == 1, rest[1:2, :], 0.0)
    ).astype(BF16)
    note_row = lax.broadcasted_iota(jnp.int32, (16, 128), 0)
    note_lane = lax.broadcasted_iota(jnp.int32, (16, 128), 1)
    own_ids = ids[...]
    facts = jnp.zeros((16, 128), F32)
    for t in range(2):
        mark = jnp.zeros((16, 128), F32)
        for j in range(8):
            mark = mark + jnp.where(note_lane == own_ids[t : t + 1, j : j + 1] + 48, 0.125, 0.0)
        keep = jnp.ones((1, 1), F32) if t == 0 else accept[...].astype(F32)
        mark = mark + jnp.where(note_lane == 65, keep, 0.0)
        facts = jnp.where(note_row == t, mark, facts)
    extra[k, :, pl.ds(7168, 128)] = facts.astype(BF16)
    e_slot = slots(1)
    send(extra.at[k], extra.at[k], e_slot, other)

    to_log2 = score_scale * log2e

    def attend(ya, yb, own):
        for yy in (ya, yb):
            for n in range(4):
                t = yy * 4 + n
                if own and yy is y:
                    t = y * 4 + (zl * 2 + k + n) % 4
                    if n == 0:
                        continue
                arrived(qbuf.at[t], q_slot + t)
        q = jnp.concatenate(
            [qbuf[pl.ds(yy * 4, 4)].reshape(128, 576) for yy in (ya, yb)], axis=0
        )
        scores = [mm(q, kc[n]) * to_log2 for n in range(2)]
        peaks = [jnp.max(part, axis=1, keepdims=True) for part in scores]
        peak = jnp.maximum(peaks[0], peaks[1])
        if own:
            row = lax.broadcasted_iota(jnp.int32, (256, 128), 0) - zl * 64
            column = lax.broadcasted_iota(jnp.int32, (256, 128), 1)
            seen = (
                (row >= 0)
                & (row < 64)
                & ((column >> 4) == (row >> 5))
                & ((column & 15) <= ((row >> 4) & 1))
            )
            own_scores = jnp.where(seen, nt(q, kn[...]) * to_log2, -jnp.inf)
            peak = jnp.maximum(peak, jnp.max(own_scores, axis=1, keepdims=True))
        denom = jnp.zeros((256, 1), F32)
        latent = jnp.zeros((256, 512), F32)
        for n in range(2):
            weights = jnp.exp2(scores[n] - peak)
            denom = denom + jnp.sum(weights, axis=1, keepdims=True)
            latent = latent + nt(weights.astype(BF16), kc[n, pl.ds(0, 512), :])
        if own:
            own_weights = jnp.exp2(own_scores - peak)
            denom = denom + jnp.sum(own_weights, axis=1, keepdims=True)
            latent = latent + mm(own_weights.astype(BF16), kn[:, pl.ds(0, 512)])
        latent = latent / denom
        level = jnp.broadcast_to(peak + jnp.log2(denom), (256, 128))
        for i, yy in enumerate((ya, yb)):
            at_rows = pl.ds(pl.multiple_of(yy * 128, 128), 128)
            for n in range(4):
                obuf[n, at_rows, :] = latent[i * 128 : i * 128 + 128, n * 128 : n * 128 + 128]
            obuf[4, at_rows, :] = level[i * 128 : i * 128 + 128]

    loads[0].wait()
    loads[1].wait()
    arrived(kn.at[pl.ds(pl.multiple_of(16 - k * 16, 16), 16)], k_slot + 1)
    arrived(kc.at[1 - k], k_slot)
    for n in (3, 4):
        loads[n].start()
    w_slot = slots(4)
    send(out_in, wout.at[own_units], w_slot + 3, other)
    attend(y, (y + 1) % 4, True)
    attend((y + 3) % 4, (y + 2) % 4, False)

    for n in (5, 6, 7):
        loads[n].start()
    send(gate_in, wgate.at[k], w_slot, other)
    send(up_in, wup.at[k], w_slot + 1, other)
    send(down_in, wdown.at[own_units], w_slot + 2, other)

    targets = assign[...]
    places = ((targets >> 1) & 1) * 16 + (targets >> 2) * 2 + (targets & 1)
    move = (lax.broadcasted_iota(jnp.int32, (32, 32), 0) == places).astype(BF16)
    spots = lax.broadcasted_iota(jnp.int32, (1, 32), 1)

    lane32 = lax.broadcasted_iota(jnp.int32, (32, 128), 1)
    v_slot = slots(8)
    own_share = (chip // 4) == k
    loads[2].wait()
    for r in (2, 1, 3, 0):
        local_chip = (chip + r) % 4
        there = k * 4 + local_chip
        stats = jnp.zeros((32, 128), F32)
        shares = []
        for j in range(4):
            head = local_chip * 4 + j
            mine = [obuf[n, pl.ds(head, 32, stride=16), :] for n in range(5)]
            latent = jnp.concatenate(mine[:4], axis=1).astype(BF16)
            shares.append(mm(latent, wuv[head]).astype(BF16))
            level = mine[4]
            high = level.astype(BF16).astype(F32)
            middle = (level - high).astype(BF16).astype(F32)
            low = level - high - middle
            stats = jnp.where(lane32 == j * 32, high, stats)
            stats = jnp.where(lane32 == j * 32 + 1, middle, stats)
            stats = jnp.where(lane32 == j * 32 + 2, low, stats)
        message = jnp.concatenate(shares + [stats.astype(BF16)], axis=1)
        vsend[r] = mm(move, message).astype(BF16).reshape(2, 16, 640)
        send(vsend.at[r, 1 - k], vrecv.at[chip], v_slot + chip, member(there * 2 + 1 - k))
        if r:
            send(vsend.at[r, k], vrecv.at[chip], v_slot + chip, member(there * 2 + k))
    own_send = pltpu.make_async_remote_copy(
        src_ref=vsend.at[0, k],
        dst_ref=vrecv.at[chip],
        send_sem=load_sem.at[8],
        recv_sem=recv_sem.at[v_slot + chip],
        device_id=member((k * 4 + chip % 4) * 2 + k),
        device_id_type=MESH,
    )

    @pl.when(own_share)
    def _():
        vrecv[chip] = vsend[0, k]

    @pl.when(jnp.logical_not(own_share))
    def _():
        own_send.start()

    for r in range(1, 8):
        c = (chip + r) % 8
        arrived(vrecv.at[c], v_slot + c)

    @pl.when(jnp.logical_not(own_share))
    def _():
        arrived(vrecv.at[chip], v_slot + chip)
        own_send.wait_send()

    lane3 = lax.broadcasted_iota(jnp.int32, (8, 16, 128), 2)
    got = vrecv[:, :, pl.ds(512, 128)].astype(F32)
    values = []
    for j in range(4):
        inside = (lane3 >= j * 32) & (lane3 < j * 32 + 3)
        level = jnp.sum(jnp.where(inside, got, 0.0), axis=2, keepdims=True)
        share = jnp.exp2(level - jnp.max(level, axis=0, keepdims=True))
        total = jnp.sum(share, axis=0)
        heard = vrecv[:, :, pl.ds(j * 128, 128)].astype(F32)
        values.append(jnp.sum(heard * share, axis=0) / total)
    values = jnp.concatenate(values, axis=1).astype(BF16)

    a_slot = slots(8)
    loads[3].wait()
    arrived(wout.at[pl.ds(pl.multiple_of(256 - k * 256, 256), 256)], w_slot + 3)
    arrived(extra.at[1 - k], e_slot)
    row_wide = lax.broadcasted_iota(jnp.int32, (16, COLS), 0)
    own_rows = []
    for kk in range(2):
        for t in range(2):
            spot = (chip * 2 + kk) * 2 + t
            place = jnp.sum(jnp.where(spots == spot, places, 0), axis=1, keepdims=True)
            own_rows.append((kk, t, place - k * 16))

    def with_extra(value, rows, columns):
        for kk in range(2):
            rest = extra[kk, :, columns].astype(F32)
            for other_kk, t, place in own_rows:
                if other_kk == kk:
                    value = value + jnp.where(rows == place, rest[t : t + 1, :], 0.0)
        return value

    facts = with_extra(jnp.zeros((16, 128), F32), note_row, pl.ds(7168, 128)).astype(BF16)
    for dy in (2, 1, 3, 0):
        for dz in (1, 0):
            c = ((y + dy) % 4) * 2 + (zl + dz) % 2
            columns = pl.ds(pl.multiple_of(c * COLS, 128), COLS)
            part = with_extra(mm(values, wout[:, columns]), row_wide, columns)
            part = jnp.concatenate([part.astype(BF16), facts], axis=1)
            if (dy, dz) == (0, 0):
                arecv[chip] = part
            else:
                n = dy * 2 + dz
                asend[n] = part
                send(asend.at[n], arecv.at[chip], a_slot + chip, member(c * 2 + k))
    for r in range(1, 8):
        c = (chip + r) % 8
        arrived(arecv.at[c], a_slot + c)
    total = jnp.sum(arecv[...].astype(F32), axis=0)
    hidden = total[:, :COLS].astype(BF16).astype(F32)
    facts = total[:, COLS:]
    keep = jnp.sum(jnp.where(note_lane == 65, facts, 0.0), axis=1, keepdims=True)

    loads[4].wait()
    gf[...] = gain[...].astype(F32)
    own_gain = jnp.concatenate([gf[pl.ds(chip * 7 + j, 1), :] for j in range(7)], axis=1)
    block = (hidden * own_gain).astype(BF16)
    squares = jnp.sum(hidden * hidden, axis=1, keepdims=True)
    squares_high = squares.astype(BF16).astype(F32)
    logits = nt(block, rpad[...])
    logits_high = logits.astype(BF16).astype(F32)
    note = logits_high + pltpu.roll(logits - logits_high, 16, 1) + facts
    note = note + jnp.where(note_lane == 32, squares_high, 0.0)
    note = note + jnp.where(note_lane == 33, squares - squares_high, 0.0)
    tail = jnp.concatenate([block[:, 768:], note.astype(BF16)], axis=1)
    gathered = (xa, xb, xc)
    for buf, (w, _, order), piece in zip(
        gathered, PIECES, (block[:, :384], block[:, 384:768], tail)
    ):
        c1, c2, c3 = (at[axis] for axis in order)
        buf[c3, c2, c1] = piece

    around = [(o1, o2) for o2 in (2, 1, 3, 0) for o1 in (2, 1, 3, 0) if (o1, o2) != (0, 0)]
    plan = []
    for buf, (w, _, order) in zip(gathered, PIECES):
        plan.append((buf, order, tuple(at[axis] for axis in order), slots(16), slots(6)))
    for o1, o2 in around:
        for buf, order, (c1, c2, c3), s1, s3 in plan:
            mine = buf.at[c3, c2, c1]
            send(mine, mine, s1 + o2 * 4 + o1, beside(order, o1, o2))

    kept = hidden * keep
    for j in range(7):
        f1[j] = kept[:, j * 128 : (j + 1) * 128]
    f2[...] = jnp.zeros_like(f2)
    for t in range(2):
        for j in range(7):
            f2[pl.ds(t * 7 + j, 8, stride=16), :] = f1[j, pl.ds(t, 8, stride=2), :]
    fsend[...] = f2[...].reshape(8, 16, 128).astype(BF16)
    f_slot = slots(8)
    for r in range(1, 8):
        c = (chip + r) % 8
        send(fsend.at[c], frecv.at[chip], f_slot + chip, member(c * 2 + k))
    frecv[chip] = fsend[chip]

    for buf, order, (c1, c2, c3), s1, s3 in plan:
        for o1, o2 in reversed(around):
            arrived(buf.at[c3, (c2 + 4 - o2) % 4, (c1 + 4 - o1) % 4], s1 + o2 * 4 + o1)

    def half(buf, c3, h, size=2):
        return buf.at[c3, pl.ds(size * h, size)]

    for h, o in ((0, 1), (1, 3), (0, 3), (1, 1)):
        for buf, order, (c1, c2, c3), s1, s3 in plan:
            mine = half(buf, c3, h)
            send(mine, mine, s3 + (0 if o == 1 else 2) + h, peer(order[2], o))

    def rows_of(n, yy, zz, columns):
        blocks = []
        for hh in range(2):
            for xx in range(4):
                c = {"x": xx, "y": yy, "z": hh * 2 + zz}
                c1, c2, c3 = (c[axis] for axis in PIECES[n][2])
                blocks.append(gathered[n][c3, c2, c1, :, columns])
        return jnp.concatenate(blocks, axis=0)

    parts = [[jnp.zeros((128, 256), F32) for _ in range(2)] for _ in range(2)]

    def multiply(n, yy, first, width):
        for zz in range(2):
            tokens = rows_of(n, yy, zz, pl.ds(0, width))
            at_rows = pl.ds(pl.multiple_of((yy * 2 + zz) * COLS + first, 128), width)
            for b in range(2):
                parts[b][0] = parts[b][0] + mm(tokens, wgate[b, at_rows, :])
                parts[b][1] = parts[b][1] + mm(tokens, wup[b, at_rows, :])

    loads[5].wait()
    loads[6].wait()
    arrived(wgate.at[1 - k], w_slot)
    arrived(wup.at[1 - k], w_slot + 1)
    multiply(0, y, 0, 384)
    for buf, order, (c1, c2, c3), s1, s3 in plan:
        for c, h, n, o in (((c3 + 3) % 4, 0, 0, 1), ((c3 + 1) % 4, 1, 3, 3)):
            view = half(buf, c, h)
            arrived(view, s3 + n)
            send(view, view, s3 + 4 + h, peer(order[2], o))

    def rest(n, last):
        buf, order, (c1, c2, c3), s1, s3 = plan[n]
        if last:
            arrived(half(buf, (c3 + 2) % 4, 0), s3 + 4)
            arrived(half(buf, (c3 + 2) % 4, 1), s3 + 5)
        else:
            arrived(half(buf, (c3 + 3) % 4, 1), s3 + 1)
            arrived(half(buf, (c3 + 1) % 4, 0), s3 + 2)

    rest(0, False)
    multiply(0, (y + 3) % 4, 0, 384)
    multiply(0, (y + 1) % 4, 0, 384)
    rest(2, False)
    rest(2, True)
    note = jnp.zeros((128, 128), F32)
    for yy in range(4):
        multiply(2, yy, 768, 128)
        for zz in range(2):
            note = note + rows_of(2, yy, zz, pl.ds(128, 128)).astype(F32)

    lane = lax.broadcasted_iota(jnp.int32, (128, 128), 1)

    def column_sum(inside):
        return jnp.sum(jnp.where(inside, note, 0.0), axis=1, keepdims=True)

    model_width = 8 * COLS
    scale = lax.rsqrt(column_sum((lane == 32) | (lane == 33)) / model_width + norm_eps)
    logits = (note + pltpu.roll(note, 112, 1)) * scale
    chosen = jnp.where(lane < 16, jax.nn.sigmoid(logits) * pltpu.roll(note, 80, 1), 0.0)
    expert = (p * 16 + s) // 8
    gate = jnp.sum(jnp.where(lane == expert, chosen, 0.0), axis=1, keepdims=True)
    gate = gate / jnp.sum(chosen, axis=1, keepdims=True) * route_scale
    gate = gate * column_sum(lane == 65) * 0.125
    rest(0, True)
    multiply(0, (y + 2) % 4, 0, 384)
    rest(1, False)
    rest(1, True)
    for yy in range(4):
        multiply(1, yy, 384, 384)
    act = [jax.nn.silu(g * scale) * (u * scale) * gate for g, u in parts]
    act = jnp.concatenate(act, axis=1).astype(BF16)
    loads[7].wait()
    arrived(wdown.at[pl.ds(pl.multiple_of(256 - k * 256, 256), 256)], w_slot + 2)
    partial = (pa, pb, pc)
    to_row = lax.broadcasted_iota(jnp.int32, (128, 128), 0)

    def project(n):
        w, order = PIECES[n][1:]
        owner = {axis: (to_row >> shift) & 3 for axis, shift in zip(order, (0, 2, 5))}
        prompt_row = ((owner["z"] >> 1) * 4 + owner["x"]) * 16
        from_row = prompt_row + (owner["y"] * 2 + (owner["z"] & 1)) * 2 + ((to_row >> 4) & 1)
        rows = mm((from_row == lane).astype(BF16), act).astype(BF16)
        start = sum(other_piece[1] for other_piece in PIECES[:n])
        for c in range(8):
            part = mm(rows, wdown[:, pl.ds(c * COLS + start, w)]).astype(BF16)
            for chunk in range(4):
                partial[n][chunk, c] = part[chunk * 32 : chunk * 32 + 32]

    plan = []
    for n, (_, w, order) in enumerate(PIECES):
        bufs = (partial[n], (r1a, r1b, r1c)[n], (r2a, r2b, r2c)[n])
        plan.append((bufs, order, tuple(at[axis] for axis in order), slots(6), slots(16)))

    def add_to(ref, *terms):
        total = ref[...].astype(F32)
        for term in terms:
            total = total + term[...].astype(F32)
        ref[...] = total.astype(BF16)

    blocks = (ba, bb, bc)

    def pass_on(piece, step):
        (part, r1, r2), order, (c1, c2, c3), s1, s2 = plan[piece]
        for n, (to, h, o) in enumerate(((2, 0, 1), (2, 1, 3), (1, 1, 1), (3, 0, 3))):
            if to == step:
                send(half(part, (c3 + step) % 4, h, 4), r1.at[n], s1 + n, peer(order[2], o))

    for n in range(3):
        project(n)
        for step in (2, 1, 3):
            pass_on(n, step)
    for n, (step, h, o) in enumerate(((1, 0, 1), (3, 1, 3))):
        for (part, r1, r2), order, (c1, c2, c3), s1, s2 in plan:
            view = half(part, (c3 + step) % 4, h, 4)
            arrived(r1.at[n], s1 + n)
            add_to(view, r1.at[n])
            send(view, r1.at[n + 4], s1 + n + 4, peer(order[2], o))
    for piece in (2, 1, 0):
        (part, r1, r2), order, (c1, c2, c3), s1, s2 = plan[piece]
        for n in (2, 3, 4, 5):
            arrived(r1.at[n], s1 + n)
        tiles = PIECES[piece][1] // 128
        for h, (one, two) in enumerate(((3, 4), (2, 5))):
            for i in range(4):
                c = h * 4 + i
                chunk = part[c3, c].astype(F32) + r1[one, i].astype(F32) + r1[two, i].astype(F32)
                for t in range(2):
                    for j in range(tiles):
                        stage[j, pl.ds(2 * c + t, 16, stride=16), :] = chunk[
                            t * 16 : t * 16 + 16, j * 128 : (j + 1) * 128
                        ]
        whole = jnp.concatenate([stage[j] for j in range(tiles)], axis=1)
        blocks[piece][...] = whole.astype(BF16).reshape(4, 4, 16, tiles * 128)
        for o1, o2 in around:
            block = blocks[piece].at[(c2 + o2) % 4, (c1 + o1) % 4]
            send(block, r2.at[o2 * 4 + o1], s2 + o2 * 4 + o1, beside(order, o1, o2))

    for r in range(1, 8):
        c = (chip + r) % 8
        arrived(frecv.at[c], f_slot + c)
    f2[...] = frecv[...].reshape(128, 128).astype(F32)

    sums = []
    for block, ((part, r1, r2), order, (c1, c2, c3), s1, s2) in zip(blocks, plan):
        for o1, o2 in reversed(around):
            arrived(r2.at[o2 * 4 + o1], s2 + o2 * 4 + o1)
        got = r2[pl.ds(1, 15)].astype(F32)
        sums.append(block[c2, c1].astype(F32) + jnp.sum(got, axis=0))
    final = jnp.concatenate(sums, axis=1)
    for j in range(7):
        f1[j] = final[:, j * 128 : (j + 1) * 128]
    rows = [
        f1[j, pl.ds(2 * c, 2), :] + f2[pl.ds(c * 16 + j, 2, stride=7), :]
        for c in range(8)
        for j in range(7)
    ]
    result[...] = jnp.concatenate(rows, axis=1).astype(BF16)
    links.finish()


def local(
    queries,
    new_keys,
    cache,
    residual,
    w_uv,
    w_out,
    norm_gain,
    router,
    expert_ids,
    w_gate,
    w_up,
    w_down,
    accept,
    assign,
):
    positions = cache.shape[1]
    whole = pl.BlockSpec(memory_space=pltpu.VMEM)
    left = pl.BlockSpec(memory_space=pl.ANY)
    scratch = [
        pltpu.VMEM((2, 576, positions), BF16),
        pltpu.VMEM((16, 512, 128), BF16),
        pltpu.VMEM((512, 7168), BF16),
        pltpu.VMEM((2, 7168, 256), BF16),
        pltpu.VMEM((2, 7168, 256), BF16),
        pltpu.VMEM((512, 7168), BF16),
        pltpu.VMEM((128, COLS), BF16),
        pltpu.VMEM((16, 2, 16, 576), BF16),
        pltpu.VMEM((128, 576), BF16),
        pltpu.VMEM((5, 512, 128), F32),
        pltpu.VMEM((4, 2, 16, 640), BF16),
        pltpu.VMEM((8, 16, 640), BF16),
        pltpu.VMEM((8, 16, COLS + 128), BF16),
        pltpu.VMEM((8, 16, COLS + 128), BF16),
        pltpu.VMEM((3, 256, 128), F32),
    ]
    scratch += [pltpu.VMEM((4, 4, 4, 16, w), BF16) for w, _, _ in PIECES]
    scratch += [pltpu.VMEM((4, 8, 32, w), BF16) for _, w, _ in PIECES]
    scratch += [pltpu.VMEM((6, 4, 32, w), BF16) for _, w, _ in PIECES]
    scratch += [pltpu.VMEM((16, 16, w), BF16) for _, w, _ in PIECES]
    scratch += [pltpu.VMEM((4, 4, 16, w), BF16) for _, w, _ in PIECES]
    scratch += [
        pltpu.VMEM((7, 16, 128), F32),
        pltpu.VMEM((128, 128), F32),
        pltpu.VMEM((8, 16, 128), BF16),
        pltpu.VMEM((8, 16, 128), BF16),
        pltpu.VMEM((56, 128), F32),
        pltpu.VMEM((2, 16, 7296), BF16),
        pltpu.SemaphoreType.DMA((9,)),
        pltpu.SemaphoreType.DMA((192,)),
        pltpu.SemaphoreType.DMA((192,)),
    ]
    rows = pl.pallas_call(
        kernel,
        out_shape=jax.ShapeDtypeStruct((2, 7168), BF16),
        in_specs=[left] * 8 + [whole] * 6,
        out_specs=whole,
        scratch_shapes=scratch,
        compiler_params=pltpu.CompilerParams(
            collective_id=0, has_side_effects=True, vmem_limit_bytes=60 * 1024 * 1024
        ),
        name="layer",
    )(
        queries,
        cache[0].T,
        w_uv,
        w_out,
        router.T,
        w_gate[0],
        w_up[0],
        w_down[0],
        new_keys,
        residual,
        norm_gain.reshape(56, 128),
        expert_ids,
        accept,
        assign,
    )
    return rows


def solution(mesh):
    placed = (
        P(("prompt", "sample"), None, None),
        P(("prompt", "sample"), None),
        P("prompt", "sample", None),
        P(("prompt", "sample"), None),
        P(),
        P("sample", None),
        P(),
        P(),
        P(("prompt", "sample"), None),
        P(("prompt", "sample"), None, None),
        P(("prompt", "sample"), None, None),
        P(("prompt", "sample"), None, None),
        P("prompt", "sample"),
        P("prompt", None),
    )
    return jax.shard_map(
        local, mesh=mesh, in_specs=placed, out_specs=P(("prompt", "sample"), None), check_vma=False
    )
```
